128 devices in a mesh: band: 4 (over y_hi, core), ga: 32 (over z, x, y_lo).
Axes of the slice: x: 4, y: 4 (y_hi: 2, y_lo: 2; y = y_hi * 2 + y_lo), z: 4, core: 2. Of those that a mesh axis runs over, the one named last changes fastest.
Arguments:
- orbitals: bfloat16 [2, 2048, 24576], P(None, 'band', 'ga'), may hold values from -0.078125 to 0.078125
- h_orbitals: bfloat16 [2, 2048, 24576], P(None, 'band', 'ga'), may hold values from -4.1875 to 4.1875
- rotation: bfloat16 [2, 2048, 2048], P(None, 'ga', 'band'), may hold values from -0.09375 to 0.09375
Outputs:
- rotated_psi: float32 [2, 2048, 24576], P(None, 'band', 'ga')
- rotated_hpsi: float32 [2, 2048, 24576], P(None, 'band', 'ga')
- subspace_h: float32 [2, 2048, 2048], P(None, 'ga', 'band')
- correlation_s: float32 [2, 2048, 2048], P(None, 'ga', 'band')
The draws below stay inside these ranges and needn't reach their ends.
All inputs are finite; a program needn't handle non-finite values.
Results may differ from the reference program's by a relative error of at most 0.0003.
Values may be sent and summed in bfloat16 or wider, within the bound.
No kernel may reach another device: no remote copies, remote signals or barrier semaphores. Data moves between devices by JAX's collectives and lax.ppermute only.
A program may use at most 128 MiB of HBM per device.

```python
import jax
import jax.numpy as jnp
from jax import lax

NB = 2048
NG = 24576
NBLK = 32
N_BAND = 4
N_GA = 32


def spiked(array, stream_key, source, target, blocks, factor):
    owner, partner = [(jnp.arange(array.shape[dim]) // (array.shape[dim] // blocks)).reshape([-1 if axis == dim else 1 for axis in range(array.ndim)]) for dim in (source, target)]
    chosen = jax.random.permutation(stream_key, blocks)[partner]
    strong = (owner == chosen) | (owner == (partner + blocks // 2) % blocks)
    return jnp.where(strong, factor * array, array)


def block_scale(rng, shape, split, low, high):
    factor_of = 1.0
    for dim, blocks in split:
        draws = jax.random.uniform(jax.random.fold_in(jax.random.fold_in(rng, 6), dim), (blocks,), jnp.float32, low / len(split), high / len(split))
        factor_of = factor_of * jnp.repeat(jnp.exp(draws), shape[dim] // blocks).reshape((-1,) + (1,) * (len(shape) - 1 - dim))
    return factor_of


def centred(stream_key, shape, width, limit, pieces=(), kind=jnp.bfloat16):
    drawn = jax.random.normal(stream_key, shape, jnp.float32) * width
    if len(pieces) > 0:
        drawn = block_scale(stream_key, shape, pieces, -0.22, 0.18) * drawn
    return jnp.clip(drawn, min=-limit, max=limit).astype(kind)


def heavy_noise(own_key, extent, width, reach, cuts, heavy, kind=jnp.bfloat16):
    drawn = width * jax.random.normal(own_key, extent, jnp.float32)
    if cuts:
        drawn = drawn * block_scale(own_key, extent, cuts, -0.22, 0.18)
    return jnp.clip(spiked(drawn, jax.random.fold_in(own_key, 3), *heavy), -reach, reach).astype(kind)


def setup_inputs(seed: int = 0) -> dict:
    key_list = jax.random.split(jax.random.key(seed), 4)
    orbitals = heavy_noise(key_list[0], (2, NB, NG), NG ** -0.5, 0.078125, ((1, 4), (2, 32)), (2, 1, 32, 2.75))
    h_orbitals = centred(key_list[1], (2, NB, NG), 0.7, 4.1875, ((1, 4), (2, 32)))
    rotation = centred(key_list[2], (2, NB, NB), (2 * NB) ** -0.5, 0.09375, ((1, 32), (2, 4)))
    return {"orbitals": orbitals, "h_orbitals": h_orbitals, "rotation": rotation}


def storage_order(total, procs, blocksize):
    index = jnp.arange(total, dtype=jnp.int32)
    index = index.reshape(total // (blocksize * procs), procs, blocksize)
    return jnp.transpose(index, (1, 0, 2)).reshape(total).astype(jnp.int32)


def mat_product(first_op, second_op):
    return jnp.dot(first_op, second_op, precision=lax.Precision.HIGHEST, preferred_element_type=jnp.float32)


def reference(orbitals, h_orbitals, rotation):
    psi_real = orbitals[0].astype(jnp.float32)
    psi_imag = orbitals[1].astype(jnp.float32)
    hpsi_real = h_orbitals[0].astype(jnp.float32)
    hpsi_imag = h_orbitals[1].astype(jnp.float32)
    row_order = storage_order(NB, N_GA, NBLK)
    col_order = storage_order(NB, N_BAND, NBLK)

    def gram(right_real, right_imag):
        real_part = mat_product(psi_real, right_real.T) + mat_product(psi_imag, right_imag.T)
        imag_part = mat_product(psi_real, right_imag.T) - mat_product(psi_imag, right_real.T)
        stacked = jnp.stack([real_part, imag_part])
        return stacked[:, row_order][:, :, col_order]

    subspace_h = gram(hpsi_real, hpsi_imag)
    correlation_s = gram(psi_real, psi_imag)
    row_inverse = jnp.argsort(row_order).astype(jnp.int32)
    col_inverse = jnp.argsort(col_order).astype(jnp.int32)
    natural = rotation[:, row_inverse][:, :, col_inverse].astype(jnp.float32)
    coef_real = natural[0]
    coef_imag = natural[1]

    def rotate(data_real, data_imag):
        real_part = mat_product(coef_real.T, data_real) - mat_product(coef_imag.T, data_imag)
        imag_part = mat_product(coef_real.T, data_imag) + mat_product(coef_imag.T, data_real)
        return jnp.stack([real_part, imag_part]).astype(jnp.float32)

    rotated_psi = rotate(psi_real, psi_imag)
    rotated_hpsi = rotate(hpsi_real, hpsi_imag)
    return rotated_psi, rotated_hpsi, subspace_h, correlation_s
```

```python
import jax
import jax.numpy as jnp
from jax import lax
from jax.sharding import PartitionSpec as P

NBLK = 32
H_SCALE = 64.0
S_SCALE = 4096.0


def place(device):
    band, ga = divmod(device, 32)
    y_hi, core = divmod(band, 2)
    z, rest = divmod(ga, 8)
    x, y_lo = divmod(rest, 2)
    return [z, x, y_lo, y_hi, core]


def device_at(z, x, y_lo, y_hi, core):
    return (y_hi * 2 + core) * 32 + z * 8 + x * 2 + y_lo


def move(value, dz=0, dx=0, y_lo=0, y_hi=0, core=0):
    pairs = []
    for source in range(128):
        z, x, low, high, c = place(source)
        target = device_at((z + dz) % 4, (x + dx) % 4, low ^ y_lo, high ^ y_hi, c ^ core)
        pairs.append((source, target))
    return lax.ppermute(value, ("band", "ga"), pairs)


def pick(stacked, index):
    return lax.dynamic_index_in_dim(stacked, index, 0, keepdims=False)


def dot_rows(left, right):
    return lax.dot_general(left, right, (((1,), (1,)), ((), ())), preferred_element_type=jnp.float32)


def planes_side_by_side(block):
    return jnp.concatenate([block[0], block[1]], axis=1)


def shards(psi, hpsi, rot):
    band = lax.axis_index("band")
    ga = lax.axis_index("ga")
    y_hi, core = band // 2, band % 2
    mz, mx, y_lo = ga // 8, (ga // 2) % 4, ga % 2

    psi_mate = move(psi, core=1)
    psi_cross = move(psi, y_hi=1)
    hpsi_mate = move(hpsi, core=1)
    hpsi_cross = move(hpsi, y_hi=1)
    psi_cross_mate = move(psi_cross, core=1)
    hpsi_cross_mate = move(hpsi_cross, core=1)

    chunks = rot.reshape(2, 64, 4, 128)

    def chunk_for(k):
        return lax.dynamic_index_in_dim(chunks, band ^ k, 2, keepdims=False)

    arrived = jnp.stack([
        chunk_for(0),
        move(chunk_for(1), core=1),
        move(chunk_for(2), y_hi=1),
        move(chunk_for(3), core=1, y_hi=1),
    ])
    by_band = jnp.stack([pick(arrived, b ^ band) for b in range(4)])
    other = move(by_band, y_lo=1)
    pair = jnp.stack([by_band, other])
    pair = jnp.stack([pick(pair, y_lo), pick(pair, 1 - y_lo)])
    xs = jnp.stack([pair, move(pair, dx=-1), move(pair, dx=2), move(pair, dx=1)])
    xs = jnp.stack([pick(xs, (n - mx) % 4) for n in range(4)])
    xs = xs.reshape(4, 2, 4, 2, 2, 32, 128)
    mine = jnp.transpose(xs, (3, 4, 2, 6, 0, 1, 5)).reshape(2, 2, 512, 256)
    up = move(mine, dz=-1)
    down = move(mine, dz=1)
    far = jnp.stack([move(down[0], dz=1), move(up[1], dz=-1)])
    zs = jnp.stack([mine, up, far, down])

    def right_rows(block):
        rows = block.reshape(2, 4, 4, 32, 768).swapaxes(1, 2).reshape(2, 512, 768)
        return rows[0], rows[1]

    h_r, h_i = right_rows(hpsi * jnp.bfloat16(H_SCALE))
    p_r, p_i = right_rows(psi * jnp.bfloat16(S_SCALE))
    right_x = jnp.concatenate([
        jnp.concatenate([h_r, h_i], axis=1),
        jnp.concatenate([h_i, -h_r], axis=1),
        jnp.concatenate([p_r, p_i], axis=1),
    ], axis=0)
    right_z = jnp.concatenate([p_i, -p_r], axis=1)

    def z_slot(z):
        return ((z // 2) ^ core) * 2 + z % 2

    def reduced(first, second):
        left = jnp.concatenate([planes_side_by_side(first), planes_side_by_side(second)], axis=0)
        by_x = left.reshape(4, 4, 64, 1536)
        by_z = left.reshape(4, 256, 1536)

        def left_for_x(d):
            return lax.dynamic_index_in_dim(by_x, (mx + d) % 4, 1, keepdims=False).reshape(256, 1536)

        def left_for_z(d):
            return pick(by_z, z_slot((mz + d) % 4))

        def part_x(d):
            return dot_rows(left_for_x(d), right_x).astype(jnp.float16)

        def part_z(d):
            return dot_rows(left_for_z(d), right_z).astype(jnp.float16)

        got_x = [move(part_x(d), dx=d) for d in (1, 3, 2)]
        got_z = [move(part_z(d), dz=d) for d in (1, 3, 2)]
        sum_x = dot_rows(left_for_x(0), right_x)
        for g in got_x:
            sum_x = sum_x + g.astype(jnp.float32)
        sum_z = dot_rows(left_for_z(0), right_z)
        for g in got_z:
            sum_z = sum_z + g.astype(jnp.float32)
        sum_x = sum_x.reshape(4, 64, 1536)
        sum_z = sum_z.reshape(4, 64, 512)
        total_x = pick(sum_x, z_slot(mz))
        for d in (1, 3, 2):
            total_x = total_x + move(pick(sum_x, z_slot((mz + d) % 4)), dz=d)
        total_z = pick(sum_z, mx)
        for d in (1, 3, 2):
            total_z = total_z + move(pick(sum_z, (mx + d) % 4), dx=d)
        total = jnp.concatenate([total_x, total_z], axis=1).reshape(2, 32, 2048)
        return pick(total, y_lo) + move(pick(total, 1 - y_lo), y_lo=1)

    near = reduced(psi, psi_mate)
    away = reduced(psi_cross, psi_cross_mate)
    halves = jnp.stack([near, away])
    halves = jnp.stack([pick(halves, y_hi), pick(halves, 1 - y_hi)])
    halves = halves.reshape(2, 32, 4, 4, 128)

    def columns_for(k):
        return lax.dynamic_index_in_dim(halves, band ^ k, 3, keepdims=False)

    cols = jnp.stack([
        columns_for(0),
        move(columns_for(1), core=1),
        move(columns_for(2), y_hi=1),
        move(columns_for(3), core=1, y_hi=1),
    ])
    cols = jnp.stack([pick(cols, q ^ band) for q in range(4)])
    mats = jnp.transpose(cols, (3, 1, 2, 0, 4)).reshape(4, 64, 512)
    subspace_h = mats[0:2] * jnp.float32(1.0 / H_SCALE)
    correlation_s = mats[2:4] * jnp.float32(1.0 / S_SCALE)

    def weights(h, c):
        parts = [pick(pick(zs, (2 * c + n - mz) % 4).swapaxes(0, 1), h) for n in range(2)]
        a = jnp.concatenate(parts, axis=2)
        a = a.reshape(2, 4, 4, 32, 512).swapaxes(1, 2).reshape(2, 512, 512)
        return jnp.concatenate([
            jnp.concatenate([a[0], -a[1]], axis=1),
            jnp.concatenate([a[1], a[0]], axis=1),
        ], axis=0)

    w = [weights(y_hi, core), weights(y_hi, 1 - core), weights(1 - y_hi, core), weights(1 - y_hi, 1 - core)]

    def rotate(blocks):
        out = None
        for weight, block in zip(w, blocks):
            term = jnp.dot(weight, block.reshape(1024, 768), preferred_element_type=jnp.float32)
            out = term if out is None else out + term
        return out.reshape(2, 512, 768)

    rotated_psi = rotate([psi, psi_mate, psi_cross, psi_cross_mate])
    rotated_hpsi = rotate([hpsi, hpsi_mate, hpsi_cross, hpsi_cross_mate])
    return rotated_psi, rotated_hpsi, subspace_h, correlation_s


def solution(mesh):
    placed = (P(None, "band", "ga"), P(None, "band", "ga"), P(None, "ga", "band"))
    return jax.shard_map(
        shards,
        mesh=mesh,
        in_specs=placed,
        out_specs=(
            P(None, "band", "ga"),
            P(None, "band", "ga"),
            P(None, "ga", "band"),
            P(None, "ga", "band"),
        ),
        check_vma=False,
    )
```

```python
import functools

import jax
import jax.numpy as jnp
from jax import lax
from jax.experimental import pallas as pl
from jax.experimental.pallas import tpu as pltpu
from jax.sharding import PartitionSpec as P

H_SCALE = 64.0
S_SCALE = 4096.0
MIB = 1024 * 1024
VMEM = pl.BlockSpec(memory_space=pltpu.VMEM)
SMEM = pl.BlockSpec(memory_space=pltpu.SMEM)


def place(device):
    band, ga = divmod(device, 32)
    y_hi, core = divmod(band, 2)
    z, rest = divmod(ga, 8)
    x, y_lo = divmod(rest, 2)
    return [z, x, y_lo, y_hi, core]


def device_at(z, x, y_lo, y_hi, core):
    return (y_hi * 2 + core) * 32 + z * 8 + x * 2 + y_lo


def move(value, dz=0, dx=0, y_lo=0, y_hi=0, core=0):
    pairs = []
    for source in range(128):
        z, x, low, high, c = place(source)
        target = device_at((z + dz) % 4, (x + dx) % 4, low ^ y_lo, high ^ y_hi, c ^ core)
        pairs.append((source, target))
    return lax.ppermute(value, ("band", "ga"), pairs)


def dot_rows(left, right):
    return lax.dot_general(left, right, (((1,), (1,)), ((), ())), preferred_element_type=jnp.float32)


def where_am_i(at):
    return at[0], at[1], at[2], at[3], at[4]


def call(kernel, outs, *args, limit=24, flops=0, **kw):
    moved = sum(a.size * a.dtype.itemsize for a in args)
    moved += sum(o.size * o.dtype.itemsize for o in jax.tree.leaves(outs))
    return pl.pallas_call(
        kernel,
        out_shape=outs,
        compiler_params=pltpu.CompilerParams(vmem_limit_bytes=limit * MIB),
        cost_estimate=pl.CostEstimate(flops=flops, bytes_accessed=moved, transcendentals=0),
        **kw,
    )(*args)


def split_kernel(at, own, other, first, second, third, fourth):
    mz, mx, y_lo, y_hi, core = where_am_i(at)
    for k, out in enumerate((first, second, third, fourth)):
        band = (y_hi * 2 + core) ^ k
        cols = pl.ds(pl.multiple_of(band * 128, 128), 128)
        out[y_lo] = own[:, :, cols]
        out[1 - y_lo] = other[:, :, cols]


def turn_kernel(at, first, second, third, fourth, out):
    mz, mx, y_lo, y_hi, core = where_am_i(at)
    for k, src in enumerate((first, second, third, fourth)):
        band = (y_hi * 2 + core) ^ k
        rows = jnp.concatenate(
            [src[low, c, h * 32:h * 32 + 32, :] for h in range(2) for c in range(2) for low in range(2)], axis=0)
        turned = rows.astype(jnp.float32).T.astype(jnp.bfloat16)
        for g in range(4):
            out[pl.ds(pl.multiple_of(g * 128 + band * 32, 32), 32), :] = turned[g * 32:g * 32 + 32, :]


def right_kernel(at, psi, psi_mate, hpsi, hpsi_mate, out):
    mz, mx, y_lo, y_hi, core = where_am_i(at)
    for half in range(2):
        band = (y_hi ^ half) * 2 + core
        for m, pair in enumerate(((hpsi, hpsi_mate), (psi, psi_mate))):
            for c, src in enumerate(pair):
                for g in range(4):
                    rows = pl.ds(pl.multiple_of(g * 128 + band * 32, 32), 32)
                    re, im = src[0, rows, :], src[1, rows, :]
                    base = half * 1024 + m * 512 + c * 128 + g * 32
                    out[base:base + 32, 0:768] = re
                    out[base:base + 32, 768:1536] = im
                    out[base + 256:base + 288, 0:768] = im
                    out[base + 256:base + 288, 768:1536] = -re


def left_kernel(x_first, at, near, other, *outs):
    mz, mx, y_lo, y_hi, core = where_am_i(at)
    for dz in range(4):
        z = (mz + dz) & 3
        is_near = (z >> 1) == core
        for dx in range(4):
            x = (mx + dx) & 3
            out = outs[dx] if x_first else outs[dz]
            for dy in range(2):
                base = (dz if x_first else dx) * 64 + dy * 32
                rows = pl.ds(pl.multiple_of((z & 1) * 256 + x * 64 + (y_lo ^ dy) * 32, 32), 32)
                for c in range(2):
                    value = jnp.where(is_near, near[c, rows, :], other[c, rows, :])
                    out[base:base + 32, c * 768:c * 768 + 768] = value


def rotate_kernel(pairs, has_acc, at, coef, *refs):
    mz, mx, y_lo, y_hi, core = where_am_i(at)
    blocks = refs[:2 * pairs]
    acc = refs[2 * pairs] if has_acc else None
    out, left, right_re, right_im = refs[-4:]

    @pl.when(pl.program_id(0) == 0)
    def _():
        for n in range(pairs):
            h = y_hi if (n == 0 and not has_acc) else 1 - y_hi
            for zx in range(16):
                left[:, n * 2048 + zx * 128:n * 2048 + zx * 128 + 128] = coef[
                    zx * 512:zx * 512 + 512, pl.ds(pl.multiple_of(h * 128, 128), 128)]

    for n in range(pairs):
        near, other = blocks[2 * n], blocks[2 * n + 1]
        for z in range(4):
            is_near = (z >> 1) == core
            for x in range(4):
                src = (z & 1) * 256 + x * 64
                base = n * 2048 + (z * 4 + x) * 128
                re = jnp.where(is_near, near[0, src:src + 64, :], other[0, src:src + 64, :])
                im = jnp.where(is_near, near[1, src:src + 64, :], other[1, src:src + 64, :])
                right_re[base:base + 64, :] = re
                right_re[base + 64:base + 128, :] = -im
                right_im[base:base + 64, :] = im
                right_im[base + 64:base + 128, :] = re
    for part, right in enumerate((right_re, right_im)):
        value = jnp.dot(left[...], right[...], preferred_element_type=jnp.float32)
        if has_acc:
            value = value + acc[part]
        out[part] = value


def rotate(at, coef, blocks, acc=None):
    pairs = len(blocks) // 2
    depth = 2048 * pairs
    tile = pl.BlockSpec((2, 512, 256), lambda n: (0, 0, n))
    whole = pl.BlockSpec((8192, 256), lambda n: (0, 0))
    args = [at, coef, *blocks] + ([acc] if acc is not None else [])
    return call(
        functools.partial(rotate_kernel, pairs, acc is not None),
        jax.ShapeDtypeStruct((2, 512, 768), jnp.float32),
        *args,
        limit=44,
        flops=2 * 1024 * depth * 768,
        grid=(3,),
        in_specs=[SMEM, whole] + [tile] * (len(args) - 2),
        out_specs=tile,
        scratch_shapes=[
            pltpu.VMEM((512, depth), jnp.bfloat16),
            pltpu.VMEM((depth, 256), jnp.bfloat16),
            pltpu.VMEM((depth, 256), jnp.bfloat16),
        ],
    )


def final_kernel(at, near, away, near_got, away_got, h_out, s_out):
    mz, mx, y_lo, y_hi, core = where_am_i(at)
    pieces = ((near, y_hi, y_hi), (away, 1 - y_hi, y_hi), (near_got, 1 - y_hi, 1 - y_hi), (away_got, y_hi, 1 - y_hi))
    for src, h, col_half in pieces:
        rows = pl.ds(pl.multiple_of(h * 32, 32), 32)
        for m in range(4):
            out, scale = (h_out, 1.0 / H_SCALE) if m < 2 else (s_out, 1.0 / S_SCALE)
            for c in range(2):
                cols = pl.ds(pl.multiple_of((col_half * 2 + (core ^ c)) * 128, 128), 128)
                out[m % 2, rows, cols] = src[:, m * 256 + c * 128:m * 256 + c * 128 + 128] * scale


def shards(psi, hpsi, rot):
    band = lax.axis_index("band")
    ga = lax.axis_index("ga")
    y_hi, core = band >> 1, band & 1
    mz, mx, y_lo = ga >> 3, (ga >> 1) & 3, ga & 1
    at = jnp.stack([mz, mx, y_lo, y_hi, core]).astype(jnp.int32)

    rot_other = move(rot, y_lo=1)
    psi_cross = move(psi, y_hi=1)
    psi_mate = move(psi, core=1)
    hpsi_mate = move(hpsi, core=1)
    hpsi_cross = move(hpsi, y_hi=1)

    sent = call(split_kernel, [jax.ShapeDtypeStruct((2, 2, 64, 128), jnp.bfloat16)] * 4, at, rot, rot_other,
                in_specs=[SMEM, VMEM, VMEM], out_specs=[VMEM] * 4)
    got = [sent[0], move(sent[1], core=1), move(sent[2], y_hi=1), move(sent[3], core=1, y_hi=1)]
    turned = call(turn_kernel, jax.ShapeDtypeStruct((512, 256), jnp.bfloat16), at, *got,
                  in_specs=[SMEM] + [VMEM] * 4, out_specs=VMEM)
    groups = [[z * 8 + x * 2 + low for z in range(4) for x in range(4)] for low in range(2)]
    coef = lax.all_gather(turned, "ga", axis=0, tiled=True, axis_index_groups=groups)

    right = call(right_kernel, jax.ShapeDtypeStruct((2048, 1536), jnp.bfloat16), at, psi, psi_mate, hpsi, hpsi_mate,
                 limit=32, in_specs=[SMEM] + [VMEM] * 4, out_specs=VMEM)
    column = lax.broadcasted_iota(jnp.int32, (1, 2048), 1)
    scale = jnp.where((column & 1023) < 512, H_SCALE, S_SCALE).astype(jnp.float32)

    def reduced(x_first, first, second):
        left = call(functools.partial(left_kernel, x_first), [jax.ShapeDtypeStruct((256, 1536), jnp.bfloat16)] * 4,
                    at, first, second, in_specs=[SMEM, VMEM, VMEM], out_specs=[VMEM] * 4)
        one, two = ("dx", "dz") if x_first else ("dz", "dx")
        got = [move((dot_rows(left[d], right) * scale).astype(jnp.float16), **{one: d}) for d in (1, 3, 2)]
        total = dot_rows(left[0], right) * scale
        for g in got:
            total = total + g.astype(jnp.float32)
        mine = total[0:64]
        for d in (1, 3, 2):
            mine = mine + move(total[d * 64:d * 64 + 64], **{two: d})
        return mine[0:32] + move(mine[32:64], y_lo=1)

    near = reduced(True, psi, psi_mate)
    psi_cross_mate = move(psi_cross, core=1)
    away = reduced(False, psi_cross, psi_cross_mate)
    hpsi_cross_mate = move(hpsi_cross, core=1)
    near_got = move(near[:, 1024:2048], y_hi=1)
    away_got = move(away[:, 1024:2048], y_hi=1)
    half = jax.ShapeDtypeStruct((2, 64, 512), jnp.float32)
    subspace_h, correlation_s = call(
        final_kernel, [half, half], at, near[:, 0:1024], away[:, 0:1024], near_got, away_got,
        in_specs=[SMEM] + [VMEM] * 4, out_specs=[VMEM] * 2)

    rotated_psi = rotate(at, coef, [psi, psi_mate, psi_cross, psi_cross_mate])
    hpsi_near = rotate(at, coef, [hpsi, hpsi_mate])
    rotated_hpsi = rotate(at, coef, [hpsi_cross, hpsi_cross_mate], hpsi_near)
    return rotated_psi, rotated_hpsi, subspace_h, correlation_s


def solution(mesh):
    placed = (P(None, "band", "ga"), P(None, "band", "ga"), P(None, "ga", "band"))
    return jax.shard_map(
        shards,
        mesh=mesh,
        in_specs=placed,
        out_specs=(
            P(None, "band", "ga"),
            P(None, "band", "ga"),
            P(None, "ga", "band"),
            P(None, "ga", "band"),
        ),
        check_vma=False,
    )
```

```python
import functools

import jax
import jax.numpy as jnp
from jax import lax
from jax.experimental import pallas as pl
from jax.experimental.pallas import tpu as pltpu
from jax.sharding import PartitionSpec as P

H_SCALE = 16.0
S_SCALE = 1024.0
MIB = 1024 * 1024
VMEM = pl.BlockSpec(memory_space=pltpu.VMEM)
SMEM = pl.BlockSpec(memory_space=pltpu.SMEM)


def place(device):
    band, ga = divmod(device, 32)
    y_hi, core = divmod(band, 2)
    z, rest = divmod(ga, 8)
    x, y_lo = divmod(rest, 2)
    return [z, x, y_lo, y_hi, core]


def device_at(z, x, y_lo, y_hi, core):
    return (y_hi * 2 + core) * 32 + z * 8 + x * 2 + y_lo


def move(value, dz=0, dx=0, y_lo=0, y_hi=0, core=0):
    pairs = []
    for source in range(128):
        z, x, low, high, c = place(source)
        target = device_at((z + dz) % 4, (x + dx) % 4, low ^ y_lo, high ^ y_hi, c ^ core)
        pairs.append((source, target))
    return lax.ppermute(value, ("band", "ga"), pairs)


def dot_rows(left, right):
    return lax.dot_general(left, right, (((1,), (1,)), ((), ())), preferred_element_type=jnp.float32)


def where_am_i(at):
    return at[0], at[1], at[2], at[3], at[4]


def call(kernel, outs, *args, limit=24, **kw):
    return pl.pallas_call(
        kernel,
        out_shape=outs,
        compiler_params=pltpu.CompilerParams(vmem_limit_bytes=limit * MIB),
        cost_estimate=pl.CostEstimate(flops=1024, bytes_accessed=1024, transcendentals=0),
        **kw,
    )(*args)


def split_kernel(at, own, other, first, second, third, fourth):
    mz, mx, y_lo, y_hi, core = where_am_i(at)
    for k, out in enumerate((first, second, third, fourth)):
        band = (y_hi * 2 + core) ^ k
        cols = pl.ds(pl.multiple_of(band * 128, 128), 128)
        out[y_lo] = own[:, :, cols]
        out[1 - y_lo] = other[:, :, cols]


def turn_kernel(at, first, second, third, fourth, out):
    mz, mx, y_lo, y_hi, core = where_am_i(at)
    for k, src in enumerate((first, second, third, fourth)):
        band = (y_hi * 2 + core) ^ k
        rows = jnp.concatenate(
            [src[low, c, h * 32:h * 32 + 32, :] for h in range(2) for c in range(2) for low in range(2)], axis=0)
        turned = rows.astype(jnp.float32).T.astype(jnp.bfloat16)
        for g in range(4):
            out[pl.ds(pl.multiple_of(g * 128 + band * 32, 32), 32), :] = turned[g * 32:g * 32 + 32, :]


def merge_kernel(at, first, second, third, fourth, out, pieces):
    mz, mx, y_lo, y_hi, core = where_am_i(at)
    for d, src in enumerate((first, second, third, fourth)):
        pieces[d] = src[...]
    for part in range(4):
        blocks = [pieces[(x - mx) & 3, :, part * 64:part * 64 + 64] for x in range(4)]
        out[:, part * 256:part * 256 + 256] = jnp.concatenate(blocks, axis=1)


def right_kernel(at, psi, psi_mate, hpsi, hpsi_mate, out):
    mz, mx, y_lo, y_hi, core = where_am_i(at)
    for half in range(2):
        band = (y_hi ^ half) * 2 + core
        for m, pair in enumerate(((hpsi, hpsi_mate), (psi, psi_mate))):
            for c, src in enumerate(pair):
                for g in range(4):
                    rows = pl.ds(pl.multiple_of(g * 128 + band * 32, 32), 32)
                    re, im = src[0, rows, :], src[1, rows, :]
                    base = m * 1024 + half * 512 + c * 128 + g * 32
                    out[base:base + 32, 0:768] = re
                    out[base:base + 32, 768:1536] = im
                    out[base + 256:base + 288, 0:768] = im
                    out[base + 256:base + 288, 768:1536] = -re


def left_kernel(both, at, near_re, near_im, other_re, other_im, *outs):
    mz, mx, y_lo, y_hi, core = where_am_i(at)
    for dz in range(4):
        z = (mz + dz) & 3
        is_near = (z >> 1) == core
        for dx in range(4):
            x = (mx + dx) & 3
            for dy in range(2):
                rows = pl.ds(pl.multiple_of((z & 1) * 256 + x * 64 + (y_lo ^ dy) * 32, 32), 32)
                by_x, by_z = dz * 64 + dy * 32, dx * 64 + dy * 32
                for c, (near, other) in enumerate(((near_re, other_re), (near_im, other_im))):
                    value = jnp.where(is_near, near[rows, :], other[rows, :])
                    outs[dx][by_x:by_x + 32, c * 768:c * 768 + 768] = value
                    if both:
                        outs[4 + dz][by_z:by_z + 32, c * 768:c * 768 + 768] = value


def whole_left_kernel(both, at, near, other, *outs):
    left_kernel(both, at, near.at[0], near.at[1], other.at[0], other.at[1], *outs)


def rotate_kernel(early, at, z0, z1, z3, *refs):
    mz, mx, y_lo, y_hi, core = where_am_i(at)
    out = refs[-1]
    if early:
        pairs = ((y_hi, refs[0:2], refs[2:4], ((0, z0), (1, z1), (3, z3))),)
        total = None
    else:
        far0, far1, acc = refs[0], refs[1], refs[10]
        pairs = ((y_hi, refs[2:4], refs[4:6], ((2, None),)),
                 (1 - y_hi, refs[6:8], refs[8:10], ((0, z0), (1, z1), (2, None), (3, z3))))
        total = jnp.concatenate([acc[0], acc[1]], axis=0)
    for h, near, other, pieces in pairs:
        for dz, piece in pieces:
            z = (mz + dz) & 3
            is_near = (z >> 1) == core
            rows = pl.ds(pl.multiple_of((z & 1) * 256, 256), 256)
            if piece is None:
                coef = jnp.where(h == 0, far0[...], far1[...])
                re, im = coef[:, 0:256], coef[:, 256:512]
            else:
                re = piece[:, pl.ds(pl.multiple_of(h * 512, 512), 256)]
                im = piece[:, pl.ds(pl.multiple_of(h * 512 + 256, 256), 256)]
            left = jnp.concatenate([
                jnp.concatenate([re, -im], axis=1),
                jnp.concatenate([im, re], axis=1),
            ], axis=0)
            right = jnp.concatenate([
                jnp.where(is_near, near[0][rows, :], other[0][rows, :]),
                jnp.where(is_near, near[1][rows, :], other[1][rows, :]),
            ], axis=0)
            term = jnp.dot(left, right, preferred_element_type=jnp.float32)
            total = term if total is None else total + term
    size = total.shape[0] // 2
    for part in range(2):
        out[part] = total[part * size:part * size + size]


def rotate(at, pieces, blocks, acc=None, rows=None):
    step = 256
    first, steps = (0, 512 // step) if rows is None else (rows * 256 // step, 256 // step)
    tile = pl.BlockSpec((2, step, 768), lambda n: (0, n + first, 0))
    plane = [pl.BlockSpec((pl.squeezed, 512, 768), lambda n, c=c: (c, 0, 0)) for c in range(2)]
    args = [at, *pieces]
    specs = [SMEM] + [pl.BlockSpec((step, c.shape[1]), lambda n: (n + first, 0)) for c in pieces]
    for block in blocks:
        args += block if isinstance(block, list) else [block, block]
        specs += [VMEM, VMEM] if isinstance(block, list) else plane
    if acc is not None:
        args.append(acc)
        specs.append(tile)
    return call(
        functools.partial(rotate_kernel, acc is None),
        jax.ShapeDtypeStruct((2, 512, 768), jnp.float32),
        *args,
        limit=20 if acc is None else 32,
        grid=(steps,),
        in_specs=specs,
        out_specs=tile,
        input_output_aliases={} if rows is None else {len(args) - 1: 0},
    )


def fold_kernel(first, h0, h1, h2, h3, keep, low):
    h = h0[...] + h1[...] + h2[...] + h3[...]
    for rows, out in ((slice(0, 32), keep), (slice(32, 64), low)):
        out[:, 0:3072] = first[rows, :]
        out[:, 3072:4096] = h[rows, :]


def part_kernel(keep, got, own, over):
    for m in range(4):
        for half, out in enumerate((own, over)):
            cols = slice(m * 1024 + half * 512, m * 1024 + half * 512 + 512)
            out[:, m * 512:m * 512 + 512] = keep[:, cols] + got[:, cols]


def final_kernel(at, own, got, h_out, s_out):
    mz, mx, y_lo, y_hi, core = where_am_i(at)
    for src, col_half in ((own, y_hi), (got, 1 - y_hi)):
        for m, out, scale, h in ((0, h_out, H_SCALE, col_half), (1, s_out, S_SCALE, col_half),
                                 (2, s_out, S_SCALE, 1 - col_half), (3, h_out, H_SCALE, 1 - col_half)):
            rows = pl.ds(pl.multiple_of(h * 32, 32), 32)
            for n in range(2):
                for c in range(2):
                    cols = pl.ds(pl.multiple_of((col_half * 2 + (core ^ c)) * 128, 128), 128)
                    base = m * 512 + n * 256 + c * 128
                    out[n, rows, cols] = src[:, base:base + 128] * (1.0 / scale)


def after(value, *earlier):
    return lax.optimization_barrier((value, *earlier))[0]


def after_all(values, *earlier):
    return list(lax.optimization_barrier((*values, *earlier))[:len(values)])


def shards(psi, hpsi, rot):
    band = lax.axis_index("band")
    ga = lax.axis_index("ga")
    y_hi, core = band >> 1, band & 1
    mz, mx, y_lo = ga >> 3, (ga >> 1) & 3, ga & 1
    at = jnp.stack([mz, mx, y_lo, y_hi, core]).astype(jnp.int32)
    column = lax.broadcasted_iota(jnp.int32, (1, 2048), 1)
    scale = jnp.where(column < 1024, H_SCALE, S_SCALE).astype(jnp.float32)

    def lefts(first, second, both):
        sizes = [256] * (8 if both else 4)
        return call(functools.partial(left_kernel, both), [jax.ShapeDtypeStruct((n, 1536), jnp.bfloat16) for n in sizes],
                    at, *first, *second, in_specs=[SMEM] + [VMEM] * 4, out_specs=[VMEM] * len(sizes))

    def for_peer(left, operand, factor):
        return (dot_rows(left, operand) * factor).astype(jnp.float16)

    def gathered(mine, operand, factor, got):
        total = dot_rows(mine, operand) * factor
        for g in got:
            total = total + g.astype(jnp.float32)
        return total

    fence = lax.optimization_barrier

    rot_other = move(rot, y_lo=1)
    psi_mate = move(psi, core=1)
    hpsi_mate = move(hpsi, core=1)
    psi, hpsi, psi_mate, hpsi_mate, rot_other = fence((psi, hpsi, psi_mate, hpsi_mate, rot_other))

    sent = call(split_kernel, [jax.ShapeDtypeStruct((2, 2, 64, 128), jnp.bfloat16)] * 4, at, rot, rot_other,
                in_specs=[SMEM, VMEM, VMEM], out_specs=[VMEM] * 4)
    got = [sent[0], move(sent[1], core=1), move(sent[2], y_hi=1), move(sent[3], core=1, y_hi=1)]
    right = call(right_kernel, jax.ShapeDtypeStruct((2048, 1536), jnp.bfloat16), at, psi, psi_mate,
                 after(hpsi, sent[0]), hpsi_mate, limit=32, in_specs=[SMEM] + [VMEM] * 4, out_specs=VMEM)
    near_left = call(functools.partial(whole_left_kernel, False), [jax.ShapeDtypeStruct((256, 1536), jnp.bfloat16)] * 4,
                     at, after(psi, right), psi_mate, in_specs=[SMEM, VMEM, VMEM], out_specs=[VMEM] * 4)
    psi, hpsi, got, right, near_left = fence((psi, hpsi, got, right, near_left))

    turned = call(turn_kernel, jax.ShapeDtypeStruct((512, 256), jnp.bfloat16), at, *got,
                  in_specs=[SMEM] + [VMEM] * 4, out_specs=VMEM)
    cross_re = move(psi[0], y_hi=1)
    xs = [turned, move(turned, dx=-1), move(turned, dx=2), move(turned, dx=1)]
    near_1 = for_peer(after(near_left[1], turned), right, scale)
    near_3 = for_peer(after(near_left[3], near_1), right, scale)
    psi, hpsi, cross_re, xs, near_1, near_3, right = fence((psi, hpsi, cross_re, xs, near_1, near_3, right))

    mine = call(merge_kernel, jax.ShapeDtypeStruct((512, 1024), jnp.bfloat16), at, *xs,
                in_specs=[SMEM] + [VMEM] * 4, out_specs=VMEM,
                scratch_shapes=[pltpu.VMEM((4, 512, 256), jnp.bfloat16)])
    near_got = [move(near_1, dx=1), move(near_3, dx=3)]
    up, down = move(mine, dz=-1), move(mine, dz=1)
    cross_im = move(psi[1], y_hi=1)
    near_2 = for_peer(after(near_left[2], mine), right, scale)
    near_own = dot_rows(after(near_left[0], near_2), right) * scale
    hpsi, cross_re, cross_im, mine, up, down, near_got, near_2, near_own, right = fence(
        (hpsi, cross_re, cross_im, mine, up, down, near_got, near_2, near_own, right))

    mate_re, mate_im = move(cross_re, core=1), move(cross_im, core=1)
    near_got.append(move(near_2, dx=2))
    down_half, up_half = down[:, 0:512], up[:, 512:1024]
    far0, far1 = move(down_half, dz=1), move(up_half, dz=-1)
    hpsi_cross = move(hpsi, y_hi=1)
    psi_cross, psi_cross_mate = [cross_re, cross_im], [mate_re, mate_im]
    away_left = lefts(psi_cross, psi_cross_mate, True)
    right_h, right_s = right[0:1024], right[1024:2048]
    h_2 = for_peer(away_left[6], right_h, H_SCALE)
    got_h = [move(h_2, dz=2)]
    h_1 = for_peer(after(away_left[5], h_2), right_h, H_SCALE)
    h_3 = for_peer(after(away_left[7], h_1), right_h, H_SCALE)
    s_1 = for_peer(after(away_left[1], h_3), right_s, S_SCALE)
    s_3 = for_peer(after(away_left[3], s_1), right_s, S_SCALE)
    s_2 = for_peer(after(away_left[2], s_3), right_s, S_SCALE)
    psi_near = rotate(at, after_all([mine, up, down], s_2), [psi, psi_mate])
    hpsi_near = rotate(at, after_all([mine, up, down], psi_near), [hpsi, hpsi_mate])
    coef = [mine, up, down, far0, far1]
    near_got, coef, h_1, h_3, s_1, s_3, s_2, got_h, right, away_left, psi_near, hpsi_near = fence(
        (near_got, coef, h_1, h_3, s_1, s_3, s_2, got_h, right, away_left, psi_near, hpsi_near))

    right_h, right_s = right[0:1024], right[1024:2048]
    got_h += [move(h_1, dz=1), move(h_3, dz=3)]
    got_s = [move(s_1, dx=1), move(s_3, dx=3), move(s_2, dx=2)]
    rotated_psi = rotate(at, coef, [psi, psi_mate, psi_cross, psi_cross_mate], psi_near)
    near_total = after(near_own, rotated_psi)
    for g in near_got:
        near_total = near_total + g.astype(jnp.float32)
    away_h = gathered(after(away_left[4], near_total), right_h, H_SCALE, got_h)
    hpsi_cross, away_h, got_s, near_total, rotated_psi, right_s = fence(
        (hpsi_cross, away_h, got_s, near_total, rotated_psi, right_s))

    hpsi_cross_mate = move(hpsi_cross, core=1)
    by_x = [away_h[0:64]] + [move(away_h[d * 64:d * 64 + 64], dx=d) for d in (1, 3, 2)]
    away_s = gathered(away_left[0], right_s, S_SCALE, got_s)
    by_z = jnp.concatenate([near_total, away_s], axis=1)
    by_z = [by_z[0:64]] + [move(by_z[d * 64:d * 64 + 64].astype(jnp.float16), dz=d) for d in (1, 3, 2)]
    first = by_z[0]
    for p in by_z[1:]:
        first = first + p.astype(jnp.float32)
    keep, low = call(fold_kernel, [jax.ShapeDtypeStruct((32, 4096), jnp.float32)] * 2, first, *by_x,
                     in_specs=[VMEM] * 5, out_specs=[VMEM] * 2)
    low_got = move(low, y_lo=1)
    blocks = [hpsi, hpsi_mate, hpsi_cross, hpsi_cross_mate]
    part_1 = rotate(at, after_all(coef, low), blocks, hpsi_near, rows=0)
    own, over = call(part_kernel, [jax.ShapeDtypeStruct((32, 2048), jnp.float32)] * 2, after(keep, part_1),
                     low_got, in_specs=[VMEM] * 2, out_specs=[VMEM] * 2)
    rotated_hpsi = rotate(at, after_all(coef, over), blocks, part_1, rows=1)
    own = after(own, rotated_hpsi)
    half = jax.ShapeDtypeStruct((2, 64, 512), jnp.float32)
    subspace_h, correlation_s = call(
        final_kernel, [half, half], at, own, move(over, y_hi=1), in_specs=[SMEM] + [VMEM] * 2, out_specs=[VMEM] * 2)
    return rotated_psi, rotated_hpsi, subspace_h, correlation_s


def solution(mesh):
    placed = (P(None, "band", "ga"), P(None, "band", "ga"), P(None, "ga", "band"))
    return jax.shard_map(
        shards,
        mesh=mesh,
        in_specs=placed,
        out_specs=(
            P(None, "band", "ga"),
            P(None, "band", "ga"),
            P(None, "ga", "band"),
            P(None, "ga", "band"),
        ),
        check_vma=False,
    )
```

```python
import functools

import jax
import jax.numpy as jnp
from jax import lax
from jax.experimental import pallas as pl
from jax.experimental.pallas import tpu as pltpu
from jax.sharding import PartitionSpec as P

ROOM = 8192.0
TINY = 1e-30
MIB = 1024 * 1024
VMEM = pl.BlockSpec(memory_space=pltpu.VMEM)
SMEM = pl.BlockSpec(memory_space=pltpu.SMEM)


def place(device):
    band, ga = divmod(device, 32)
    y_hi, core = divmod(band, 2)
    z, rest = divmod(ga, 8)
    x, y_lo = divmod(rest, 2)
    return [z, x, y_lo, y_hi, core]


def device_at(z, x, y_lo, y_hi, core):
    return (y_hi * 2 + core) * 32 + z * 8 + x * 2 + y_lo


def move(value, dz=0, dx=0, y_lo=0, y_hi=0, core=0):
    pairs = []
    for source in range(128):
        z, x, low, high, c = place(source)
        target = device_at((z + dz) % 4, (x + dx) % 4, low ^ y_lo, high ^ y_hi, c ^ core)
        pairs.append((source, target))
    return lax.ppermute(value, ("band", "ga"), pairs)


def dot_rows(left, right):
    return lax.dot_general(left, right, (((1,), (1,)), ((), ())), preferred_element_type=jnp.float32)


def where_am_i(at):
    return at[0], at[1], at[2], at[3], at[4]


def call(kernel, outs, *args, limit=24, **kw):
    return pl.pallas_call(
        kernel,
        out_shape=outs,
        compiler_params=pltpu.CompilerParams(vmem_limit_bytes=limit * MIB),
        cost_estimate=pl.CostEstimate(flops=1024, bytes_accessed=1024, transcendentals=0),
        **kw,
    )(*args)


def split_kernel(at, largest, own, other, first, second, third, fourth):
    mz, mx, y_lo, y_hi, core = where_am_i(at)
    for k, out in enumerate((first, second, third, fourth)):
        band = (y_hi * 2 + core) ^ k
        cols = pl.ds(pl.multiple_of(band * 128, 128), 128)
        out[y_lo, :, 0:64, :] = own[:, :, cols]
        out[1 - y_lo, :, 0:64, :] = other[:, :, cols]
        tail = jnp.concatenate([jnp.full((8, 128), largest[0], jnp.float32), jnp.full((8, 128), largest[1], jnp.float32)])
        for low in range(2):
            for c in range(2):
                out[low, c, 64:80, :] = tail.astype(jnp.bfloat16)


def turn_kernel(at, first, second, third, fourth, out, scales):
    mz, mx, y_lo, y_hi, core = where_am_i(at)
    tails = []
    for k, src in enumerate((first, second, third, fourth)):
        band = (y_hi * 2 + core) ^ k
        rows = jnp.concatenate(
            [src[low, c, h * 32:h * 32 + 32, :] for h in range(2) for c in range(2) for low in range(2)], axis=0)
        turned = rows.astype(jnp.float32).T.astype(jnp.bfloat16)
        for g in range(4):
            out[pl.ds(pl.multiple_of(g * 128 + band * 32, 32), 32), :] = turned[g * 32:g * 32 + 32, :]
        tails.append(src[0, 0, 64:80, :].astype(jnp.float32))
    chip = jnp.maximum(tails[0], tails[1])
    psi = jnp.maximum(chip, jnp.maximum(tails[2], tails[3]))[0:8]
    for m, right in ((0, chip[8:16]), (1, chip[0:8])):
        factor = (ROOM / (1536.0 * psi * right + TINY)).astype(jnp.bfloat16).astype(jnp.float32)
        for n in range(8):
            scales[:, m * 1024 + n * 128:m * 1024 + n * 128 + 128] = factor
        if m == 0:
            first_factor = factor
    tail = jnp.concatenate([first_factor, factor], axis=0).astype(jnp.bfloat16)
    out[512:528, 0:128] = tail
    out[512:528, 128:256] = tail


def factor_kernel(at, x1, x2, x3, mine, up, far, down, out):
    mz, mx, y_lo, y_hi, core = where_am_i(at)
    lanes = lax.broadcasted_iota(jnp.int32, (16, 256), 1)

    def put(row, pair):
        for m in range(2):
            out[row:row + 1, m * 1024:m * 1024 + 1024] = jnp.broadcast_to(pair[m], (1, 1024))

    def pair(values):
        return values[0:1, 0:1], values[8:9, 0:1]

    for row, ref in enumerate((x3, x1, x2)):
        put(row, [1.0 / v for v in pair(ref[512:528, 0:128].astype(jnp.float32))])
    for row, ref in enumerate((down, up, far)):
        values = ref[512:528, 0:256].astype(jnp.float32)
        here = jnp.min(jnp.where((lanes >> 6) == mx, values, 3e38), axis=1, keepdims=True)
        put(3 + row, [1.0 / v for v in pair(here)])
        put(7 + row, [1.0 / v for v in pair(jnp.min(values, axis=1, keepdims=True))])
    put(6, pair(jnp.min(mine[512:528, 0:256].astype(jnp.float32), axis=1, keepdims=True)))


def merge_kernel(at, first, second, third, fourth, out, pieces):
    mz, mx, y_lo, y_hi, core = where_am_i(at)
    for d, src in enumerate((first, second, third, fourth)):
        pieces[d] = src[...]
    for part in range(4):
        blocks = [pieces[(x - mx) & 3, :, part * 64:part * 64 + 64] for x in range(4)]
        out[:, part * 256:part * 256 + 256] = jnp.concatenate(blocks, axis=1)


def right_kernel(at, psi, psi_mate, hpsi, hpsi_mate, out):
    mz, mx, y_lo, y_hi, core = where_am_i(at)
    for half in range(2):
        band = (y_hi ^ half) * 2 + core
        for m, pair in enumerate(((hpsi, hpsi_mate), (psi, psi_mate))):
            for c, src in enumerate(pair):
                for g in range(4):
                    rows = pl.ds(pl.multiple_of(g * 128 + band * 32, 32), 32)
                    re, im = src[0, rows, :], src[1, rows, :]
                    base = m * 1024 + half * 512 + c * 128 + g * 32
                    out[base:base + 32, 0:768] = re
                    out[base:base + 32, 768:1536] = im
                    out[base + 256:base + 288, 0:768] = im
                    out[base + 256:base + 288, 768:1536] = -re


def left_kernel(both, at, near_re, near_im, other_re, other_im, *outs):
    mz, mx, y_lo, y_hi, core = where_am_i(at)
    for dz in range(4):
        z = (mz + dz) & 3
        is_near = (z >> 1) == core
        for dx in range(4):
            x = (mx + dx) & 3
            for dy in range(2):
                rows = pl.ds(pl.multiple_of((z & 1) * 256 + x * 64 + (y_lo ^ dy) * 32, 32), 32)
                by_x, by_z = dz * 64 + dy * 32, dx * 64 + dy * 32
                for c, (near, other) in enumerate(((near_re, other_re), (near_im, other_im))):
                    value = jnp.where(is_near, near[rows, :], other[rows, :])
                    outs[dx][by_x:by_x + 32, c * 768:c * 768 + 768] = value
                    if both:
                        outs[4 + dz][by_z:by_z + 32, c * 768:c * 768 + 768] = value


def whole_left_kernel(both, at, near, other, *outs):
    left_kernel(both, at, near.at[0], near.at[1], other.at[0], other.at[1], *outs)


def rotate_kernel(early, at, z0, z1, z3, *refs):
    mz, mx, y_lo, y_hi, core = where_am_i(at)
    out = refs[-1]
    if early:
        pairs = ((y_hi, refs[0:2], refs[2:4], ((0, z0), (1, z1), (3, z3))),)
        total = None
    else:
        far0, far1, acc = refs[0], refs[1], refs[10]
        pairs = ((y_hi, refs[2:4], refs[4:6], ((2, None),)),
                 (1 - y_hi, refs[6:8], refs[8:10], ((0, z0), (1, z1), (2, None), (3, z3))))
        total = jnp.concatenate([acc[0], acc[1]], axis=0)
    for h, near, other, pieces in pairs:
        for dz, piece in pieces:
            z = (mz + dz) & 3
            is_near = (z >> 1) == core
            rows = pl.ds(pl.multiple_of((z & 1) * 256, 256), 256)
            if piece is None:
                coef = jnp.where(h == 0, far0[...], far1[...])
                re, im = coef[:, 0:256], coef[:, 256:512]
            else:
                re = piece[:, pl.ds(pl.multiple_of(h * 512, 512), 256)]
                im = piece[:, pl.ds(pl.multiple_of(h * 512 + 256, 256), 256)]
            left = jnp.concatenate([
                jnp.concatenate([re, -im], axis=1),
                jnp.concatenate([im, re], axis=1),
            ], axis=0)
            right = jnp.concatenate([
                jnp.where(is_near, near[0][rows, :], other[0][rows, :]),
                jnp.where(is_near, near[1][rows, :], other[1][rows, :]),
            ], axis=0)
            term = jnp.dot(left, right, preferred_element_type=jnp.float32)
            total = term if total is None else total + term
    size = total.shape[0] // 2
    for part in range(2):
        out[part] = total[part * size:part * size + size]


def rotate(at, pieces, blocks, acc=None, rows=None):
    step = 256
    first, steps = (0, 512 // step) if rows is None else (rows * 256 // step, 256 // step)
    tile = pl.BlockSpec((2, step, 768), lambda n: (0, n + first, 0))
    plane = [pl.BlockSpec((pl.squeezed, 512, 768), lambda n, c=c: (c, 0, 0)) for c in range(2)]
    args = [at, *pieces]
    specs = [SMEM] + [pl.BlockSpec((step, c.shape[1]), lambda n: (n + first, 0)) for c in pieces]
    for block in blocks:
        args += block if isinstance(block, list) else [block, block]
        specs += [VMEM, VMEM] if isinstance(block, list) else plane
    if acc is not None:
        args.append(acc)
        specs.append(tile)
    return call(
        functools.partial(rotate_kernel, acc is None),
        jax.ShapeDtypeStruct((2, 512, 768), jnp.float32),
        *args,
        limit=20 if acc is None else 32,
        grid=(steps,),
        in_specs=specs,
        out_specs=tile,
        input_output_aliases={} if rows is None else {len(args) - 1: 0},
    )


def fold_kernel(first, h0, h1, h2, h3, keep, low):
    h = h0[...] + h1[...] + h2[...] + h3[...]
    for rows, out in ((slice(0, 32), keep), (slice(32, 64), low)):
        out[:, 0:3072] = first[rows, :]
        out[:, 3072:4096] = h[rows, :]


def part_kernel(keep, got, own, over):
    for m in range(4):
        for half, out in enumerate((own, over)):
            cols = slice(m * 1024 + half * 512, m * 1024 + half * 512 + 512)
            out[:, m * 512:m * 512 + 512] = keep[:, cols] + got[:, cols]


def final_kernel(at, own, got, h_out, s_out):
    mz, mx, y_lo, y_hi, core = where_am_i(at)
    for src, col_half in ((own, y_hi), (got, 1 - y_hi)):
        for m, out, h in ((0, h_out, col_half), (1, s_out, col_half), (2, s_out, 1 - col_half), (3, h_out, 1 - col_half)):
            rows = pl.ds(pl.multiple_of(h * 32, 32), 32)
            for n in range(2):
                for c in range(2):
                    cols = pl.ds(pl.multiple_of((col_half * 2 + (core ^ c)) * 128, 128), 128)
                    base = m * 512 + n * 256 + c * 128
                    out[n, rows, cols] = src[:, base:base + 128]


def after(value, *earlier):
    return lax.optimization_barrier((value, *earlier))[0]


def after_all(values, *earlier):
    return list(lax.optimization_barrier((*values, *earlier))[:len(values)])


def shards(psi, hpsi, rot):
    band = lax.axis_index("band")
    ga = lax.axis_index("ga")
    y_hi, core = band >> 1, band & 1
    mz, mx, y_lo = ga >> 3, (ga >> 1) & 3, ga & 1
    at = jnp.stack([mz, mx, y_lo, y_hi, core]).astype(jnp.int32)

    def lefts(first, second, both):
        sizes = [256] * (8 if both else 4)
        return call(functools.partial(left_kernel, both), [jax.ShapeDtypeStruct((n, 1536), jnp.bfloat16) for n in sizes],
                    at, *first, *second, in_specs=[SMEM] + [VMEM] * 4, out_specs=[VMEM] * len(sizes))

    def for_peer(left, operand, factor):
        return (dot_rows(left, operand) * factor).astype(jnp.float16)

    def gathered(mine, operand, factors, got):
        total = dot_rows(mine, operand)
        for factor, g in zip(factors, got):
            total = total + g.astype(jnp.float32) * factor
        return total

    fence = lax.optimization_barrier

    largest = jnp.stack([jnp.max(jnp.abs(psi)), jnp.max(jnp.abs(hpsi))]).astype(jnp.float32)
    rot_other = move(rot, y_lo=1)
    psi_mate = move(psi, core=1)
    hpsi_mate = move(hpsi, core=1)
    psi, hpsi, psi_mate, hpsi_mate, rot_other = fence((psi, hpsi, psi_mate, hpsi_mate, rot_other))

    sent = call(split_kernel, [jax.ShapeDtypeStruct((2, 2, 80, 128), jnp.bfloat16)] * 4, at, largest, rot,
                rot_other, in_specs=[SMEM, SMEM, VMEM, VMEM], out_specs=[VMEM] * 4)
    got = [sent[0], move(sent[1], core=1), move(sent[2], y_hi=1), move(sent[3], core=1, y_hi=1)]
    right = call(right_kernel, jax.ShapeDtypeStruct((2048, 1536), jnp.bfloat16), at, psi, psi_mate,
                 after(hpsi, sent[0]), hpsi_mate, limit=32, in_specs=[SMEM] + [VMEM] * 4, out_specs=VMEM)
    near_left = call(functools.partial(whole_left_kernel, False), [jax.ShapeDtypeStruct((256, 1536), jnp.bfloat16)] * 4,
                     at, after(psi, right), psi_mate, in_specs=[SMEM, VMEM, VMEM], out_specs=[VMEM] * 4)
    psi, hpsi, got, right, near_left = fence((psi, hpsi, got, right, near_left))

    turned, scale = call(turn_kernel, [jax.ShapeDtypeStruct((528, 256), jnp.bfloat16),
                                       jax.ShapeDtypeStruct((8, 2048), jnp.float32)], at, *got,
                         in_specs=[SMEM] + [VMEM] * 4, out_specs=[VMEM] * 2)
    scale = scale[0:1]
    scale_h, scale_s = scale[:, 0:1024], scale[:, 1024:2048]
    cross_re = move(psi[0], y_hi=1)
    xs = [turned, move(turned, dx=-1), move(turned, dx=2), move(turned, dx=1)]
    near_1 = for_peer(after(near_left[1], turned), right, scale)
    near_3 = for_peer(after(near_left[3], near_1), right, scale)
    psi, hpsi, cross_re, near_1, near_3, right = fence((psi, hpsi, cross_re, near_1, near_3, right))
    xs, right = fence((xs, right))

    mine = call(merge_kernel, jax.ShapeDtypeStruct((528, 1024), jnp.bfloat16), at, *xs,
                in_specs=[SMEM] + [VMEM] * 4, out_specs=VMEM,
                scratch_shapes=[pltpu.VMEM((4, 528, 256), jnp.bfloat16)])
    near_got = [move(near_1, dx=1), move(near_3, dx=3)]
    up, down = move(mine, dz=-1), move(mine, dz=1)
    cross_im = move(psi[1], y_hi=1)
    near_2 = for_peer(after(near_left[2], mine), right, scale)
    near_own = dot_rows(after(near_left[0], near_2), right)
    hpsi, cross_re, mine, up, down, near_got, near_2, near_own, right = fence(
        (hpsi, cross_re, mine, up, down, near_got, near_2, near_own, right))
    cross_im, near_2, up, down = fence((cross_im, near_2, up, down))

    mate_re, mate_im = move(cross_re, core=1), move(cross_im, core=1)
    near_got.append(move(near_2, dx=2))
    down_half, up_half = down[:, 0:512], up[:, 512:1024]
    far0, far1 = move(down_half, dz=1), move(up_half, dz=-1)
    hpsi_cross = move(hpsi, y_hi=1)
    psi_cross, psi_cross_mate = [cross_re, cross_im], [mate_re, mate_im]
    away_left = lefts(psi_cross, psi_cross_mate, True)
    right_h, right_s = right[0:1024], right[1024:2048]
    h_2 = for_peer(away_left[6], right_h, scale_h)
    got_h = [move(h_2, dz=2)]
    h_1 = for_peer(after(away_left[5], h_2), right_h, scale_h)
    h_3 = for_peer(after(away_left[7], h_1), right_h, scale_h)
    s_1 = for_peer(after(away_left[1], h_3), right_s, scale_s)
    s_3 = for_peer(after(away_left[3], s_1), right_s, scale_s)
    s_2 = for_peer(after(away_left[2], s_3), right_s, scale_s)
    psi_near = rotate(at, after_all([mine, up, down], s_2), [psi, psi_mate])
    hpsi_near = rotate(at, after_all([mine, up, down], psi_near), [hpsi, hpsi_mate])
    coef = [mine, up, down, far0, far1]
    near_got, coef, h_1, h_3, s_1, s_3, s_2, got_h, right, away_left, psi_near, hpsi_near = fence(
        (near_got, coef, h_1, h_3, s_1, s_3, s_2, got_h, right, away_left, psi_near, hpsi_near))

    right_h, right_s = right[0:1024], right[1024:2048]
    got_h += [move(h_1, dz=1), move(h_3, dz=3)]
    got_s = [move(s_1, dx=1), move(s_3, dx=3), move(s_2, dx=2)]
    rotated_psi = rotate(at, coef, [psi, psi_mate, psi_cross, psi_cross_mate], psi_near)
    factors = call(factor_kernel, jax.ShapeDtypeStruct((16, 2048), jnp.float32), after(at, rotated_psi), *xs[1:], mine, up,
                   far0, down, in_specs=[SMEM] + [VMEM] * 7, out_specs=VMEM)
    factor = [factors[n:n + 1] for n in range(10)]
    near_total = near_own
    for n, g in enumerate(near_got):
        near_total = near_total + g.astype(jnp.float32) * factor[n]
    got_h = [got_h[1], got_h[2], got_h[0]]
    away_h = gathered(after(away_left[4], near_total), right_h, [f[:, 0:1024] for f in factor[3:6]], got_h)
    hpsi_cross, away_h, got_s, near_total, rotated_psi, right_s = fence(
        (hpsi_cross, away_h, got_s, near_total, rotated_psi, right_s))

    hpsi_cross_mate = move(hpsi_cross, core=1)
    by_x = [away_h[0:64]] + [move(away_h[d * 64:d * 64 + 64], dx=d) for d in (1, 3, 2)]
    away_s = gathered(away_left[0], right_s, [f[:, 1024:2048] for f in factor[0:3]], got_s)
    by_z = jnp.concatenate([near_total, away_s], axis=1)
    factor = [jnp.concatenate([f, f[:, 1024:2048]], axis=1) for f in factor[6:10]]
    by_z = [by_z[0:64]] + [move((by_z[d * 64:d * 64 + 64] * factor[0]).astype(jnp.float16), dz=d) for d in (1, 3, 2)]
    first = by_z[0]
    for p, f in zip(by_z[1:], factor[1:]):
        first = first + p.astype(jnp.float32) * f
    keep, low = call(fold_kernel, [jax.ShapeDtypeStruct((32, 4096), jnp.float32)] * 2, first, *by_x,
                     in_specs=[VMEM] * 5, out_specs=[VMEM] * 2)
    low_got = move(low, y_lo=1)
    blocks = [hpsi, hpsi_mate, hpsi_cross, hpsi_cross_mate]
    part_1 = rotate(at, after_all(coef, low), blocks, hpsi_near, rows=0)
    own, over = call(part_kernel, [jax.ShapeDtypeStruct((32, 2048), jnp.float32)] * 2, after(keep, part_1),
                     low_got, in_specs=[VMEM] * 2, out_specs=[VMEM] * 2)
    rotated_hpsi = rotate(at, after_all(coef, over), blocks, part_1, rows=1)
    own = after(own, rotated_hpsi)
    half = jax.ShapeDtypeStruct((2, 64, 512), jnp.float32)
    subspace_h, correlation_s = call(
        final_kernel, [half, half], at, own, move(over, y_hi=1), in_specs=[SMEM] + [VMEM] * 2, out_specs=[VMEM] * 2)
    return rotated_psi, rotated_hpsi, subspace_h, correlation_s


def solution(mesh):
    placed = (P(None, "band", "ga"), P(None, "band", "ga"), P(None, "ga", "band"))
    return jax.shard_map(
        shards,
        mesh=mesh,
        in_specs=placed,
        out_specs=(
            P(None, "band", "ga"),
            P(None, "band", "ga"),
            P(None, "ga", "band"),
            P(None, "ga", "band"),
        ),
        check_vma=False,
    )
```

```python
import functools

import jax
import jax.numpy as jnp
from jax import lax
from jax.experimental import pallas as pl
from jax.experimental.pallas import tpu as pltpu
from jax.sharding import PartitionSpec as P

ROOM = 8192.0
TINY = 1e-30
MIB = 1024 * 1024
VMEM = pl.BlockSpec(memory_space=pltpu.VMEM)
SMEM = pl.BlockSpec(memory_space=pltpu.SMEM)


def place(device):
    band, ga = divmod(device, 32)
    y_hi, core = divmod(band, 2)
    z, rest = divmod(ga, 8)
    x, y_lo = divmod(rest, 2)
    return [z, x, y_lo, y_hi, core]


def device_at(z, x, y_lo, y_hi, core):
    return (y_hi * 2 + core) * 32 + z * 8 + x * 2 + y_lo


def move(value, dz=0, dx=0, y_lo=0, y_hi=0, core=0):
    pairs = []
    for source in range(128):
        z, x, low, high, c = place(source)
        target = device_at((z + dz) % 4, (x + dx) % 4, low ^ y_lo, high ^ y_hi, c ^ core)
        pairs.append((source, target))
    return lax.ppermute(value, ("band", "ga"), pairs)


def dot_rows(left, right):
    return lax.dot_general(left, right, (((1,), (1,)), ((), ())), preferred_element_type=jnp.float32)


def where_am_i(at):
    return at[0], at[1], at[2], at[3], at[4]


def call(kernel, outs, *args, limit=24, **kw):
    return pl.pallas_call(
        kernel,
        out_shape=outs,
        compiler_params=pltpu.CompilerParams(vmem_limit_bytes=limit * MIB),
        cost_estimate=pl.CostEstimate(flops=1024, bytes_accessed=1024, transcendentals=0),
        **kw,
    )(*args)


def split_kernel(at, largest, own, other, first, second, third, fourth):
    mz, mx, y_lo, y_hi, core = where_am_i(at)
    for k, out in enumerate((first, second, third, fourth)):
        band = (y_hi * 2 + core) ^ k
        cols = pl.ds(pl.multiple_of(band * 128, 128), 128)
        out[y_lo, :, 0:64, :] = own[:, :, cols]
        out[1 - y_lo, :, 0:64, :] = other[:, :, cols]
        tail = jnp.concatenate([jnp.full((8, 128), largest[0], jnp.float32), jnp.full((8, 128), largest[1], jnp.float32)])
        for low in range(2):
            for c in range(2):
                out[low, c, 64:80, :] = tail.astype(jnp.bfloat16)


def turn_kernel(at, first, second, third, fourth, out, scales):
    mz, mx, y_lo, y_hi, core = where_am_i(at)
    tails = []
    for k, src in enumerate((first, second, third, fourth)):
        band = (y_hi * 2 + core) ^ k
        rows = jnp.concatenate(
            [src[low, c, h * 32:h * 32 + 32, :] for h in range(2) for c in range(2) for low in range(2)], axis=0)
        turned = rows.astype(jnp.float32).T.astype(jnp.bfloat16)
        for g in range(4):
            out[pl.ds(pl.multiple_of(g * 128 + band * 32, 32), 32), :] = turned[g * 32:g * 32 + 32, :]
        tails.append(src[0, 0, 64:80, :].astype(jnp.float32))
    chip = jnp.maximum(tails[0], tails[1])
    psi = jnp.maximum(chip, jnp.maximum(tails[2], tails[3]))[0:8]
    for m, right in ((0, chip[8:16]), (1, chip[0:8])):
        factor = (ROOM / (1536.0 * psi * right + TINY)).astype(jnp.bfloat16).astype(jnp.float32)
        for n in range(8):
            scales[:, m * 1024 + n * 128:m * 1024 + n * 128 + 128] = factor
        if m == 0:
            first_factor = factor
    tail = jnp.concatenate([first_factor, factor], axis=0).astype(jnp.bfloat16)
    out[512:528, 0:128] = tail
    out[512:528, 128:256] = tail


def factor_kernel(at, x1, x2, x3, mine, up, far, down, out):
    mz, mx, y_lo, y_hi, core = where_am_i(at)
    lanes = lax.broadcasted_iota(jnp.int32, (16, 256), 1)

    def put(row, pair):
        for m in range(2):
            out[row:row + 1, m * 1024:m * 1024 + 1024] = jnp.broadcast_to(pair[m], (1, 1024))

    def pair(values):
        return values[0:1, 0:1], values[8:9, 0:1]

    for row, ref in enumerate((x3, x1, x2)):
        put(row, [1.0 / v for v in pair(ref[512:528, 0:128].astype(jnp.float32))])
    for row, ref in enumerate((down, up, far)):
        values = ref[512:528, 0:256].astype(jnp.float32)
        here = jnp.min(jnp.where((lanes >> 6) == mx, values, 3e38), axis=1, keepdims=True)
        put(3 + row, [1.0 / v for v in pair(here)])
        put(7 + row, [1.0 / v for v in pair(jnp.min(values, axis=1, keepdims=True))])
    put(6, pair(jnp.min(mine[512:528, 0:256].astype(jnp.float32), axis=1, keepdims=True)))


def merge_kernel(at, first, second, third, fourth, out, pieces):
    mz, mx, y_lo, y_hi, core = where_am_i(at)
    for d, src in enumerate((first, second, third, fourth)):
        pieces[d] = src[...]
    for part in range(4):
        blocks = [pieces[(x - mx) & 3, :, part * 64:part * 64 + 64] for x in range(4)]
        out[:, part * 256:part * 256 + 256] = jnp.concatenate(blocks, axis=1)


def right_kernel(at, psi, psi_mate, hpsi, hpsi_mate, out):
    mz, mx, y_lo, y_hi, core = where_am_i(at)
    for half in range(2):
        band = (y_hi ^ half) * 2 + core
        for m, pair in enumerate(((hpsi, hpsi_mate), (psi, psi_mate))):
            for c, src in enumerate(pair):
                for g in range(4):
                    rows = pl.ds(pl.multiple_of(g * 128 + band * 32, 32), 32)
                    re, im = src[0, rows, :], src[1, rows, :]
                    base = m * 1024 + half * 512 + c * 128 + g * 32
                    out[base:base + 32, 0:768] = re
                    out[base:base + 32, 768:1536] = im
                    out[base + 256:base + 288, 0:768] = im
                    out[base + 256:base + 288, 768:1536] = -re


def left_kernel(both, at, *refs):
    mz, mx, y_lo, y_hi, core = where_am_i(at)
    pieces = 2 if both else 1
    nears, others, outs = refs[:pieces], refs[pieces:2 * pieces], refs[2 * pieces:]
    for dz in range(4):
        z = (mz + dz) & 3
        is_near = (z >> 1) == core
        for dx in range(4):
            x = (mx + dx) & 3
            for dy in range(2):
                rows = pl.ds(pl.multiple_of((z & 1) * 256 + x * 64 + (y_lo ^ dy) * 32, 32), 32)
                by_x, by_z = dz * 64 + dy * 32, dx * 64 + dy * 32
                for c in range(2):
                    base = c * 768
                    for near, other in zip(nears, others):
                        value = jnp.where(is_near, near[c, rows, :], other[c, rows, :])
                        cols = slice(base, base + value.shape[1])
                        base += value.shape[1]
                        outs[dx][by_x:by_x + 32, cols] = value
                        if both:
                            outs[4 + dz][by_z:by_z + 32, cols] = value


def planes(refs):
    return lambda c, rows: refs[c][rows, :]


def columns(refs):
    return lambda c, rows: jnp.concatenate([r[c, rows, :] for r in refs], axis=1)


def rotate_kernel(early, split, at, z0, z1, z3, *refs):
    mz, mx, y_lo, y_hi, core = where_am_i(at)
    out = refs[-1]
    if early:
        near, other = planes(refs[0:2]), planes(refs[2:4])
        pairs = ((y_hi, near, other, ((0, z0), (1, z1), (3, z3))),)
        total = None
    else:
        far0, far1, acc = refs[0], refs[1], refs[10]
        near, other = planes(refs[2:4]), planes(refs[4:6])
        cross = (columns if split else planes)(refs[6:8]), (columns if split else planes)(refs[8:10])
        pairs = ((y_hi, near, other, ((2, None),)),
                 (1 - y_hi, *cross, ((0, z0), (1, z1), (2, None), (3, z3))))
        total = jnp.concatenate([acc[0], acc[1]], axis=0)
    for h, near, other, pieces in pairs:
        for dz, piece in pieces:
            z = (mz + dz) & 3
            is_near = (z >> 1) == core
            rows = pl.ds(pl.multiple_of((z & 1) * 256, 256), 256)
            if piece is None:
                coef = jnp.where(h == 0, far0[...], far1[...])
                re, im = coef[:, 0:256], coef[:, 256:512]
            else:
                re = piece[:, pl.ds(pl.multiple_of(h * 512, 512), 256)]
                im = piece[:, pl.ds(pl.multiple_of(h * 512 + 256, 256), 256)]
            left = jnp.concatenate([
                jnp.concatenate([re, -im], axis=1),
                jnp.concatenate([im, re], axis=1),
            ], axis=0)
            right = jnp.concatenate([
                jnp.where(is_near, near(0, rows), other(0, rows)),
                jnp.where(is_near, near(1, rows), other(1, rows)),
            ], axis=0)
            term = jnp.dot(left, right, preferred_element_type=jnp.float32)
            total = term if total is None else total + term
    size = total.shape[0] // 2
    for part in range(2):
        out[part] = total[part * size:part * size + size]


def rotate(at, pieces, blocks, acc=None, rows=None):
    step = 256
    first, steps = (0, 512 // step) if rows is None else (rows * 256 // step, 256 // step)
    tile = pl.BlockSpec((2, step, 768), lambda n: (0, n + first, 0))
    plane = [pl.BlockSpec((pl.squeezed, 512, 768), lambda n, c=c: (c, 0, 0)) for c in range(2)]
    args = [at, *pieces]
    specs = [SMEM] + [pl.BlockSpec((step, c.shape[1]), lambda n: (n + first, 0)) for c in pieces]
    for block in blocks:
        args += block if isinstance(block, list) else [block, block]
        specs += [VMEM, VMEM] if isinstance(block, list) else plane
    if acc is not None:
        args.append(acc)
        specs.append(tile)
    return call(
        functools.partial(rotate_kernel, acc is None, isinstance(blocks[-1], list)),
        jax.ShapeDtypeStruct((2, 512, 768), jnp.float32),
        *args,
        limit=20 if acc is None else 32,
        grid=(steps,),
        in_specs=specs,
        out_specs=tile,
        input_output_aliases={} if rows is None else {len(args) - 1: 0},
    )


def fold_kernel(first, h0, h1, h2, h3, keep, low):
    h = h0[...] + h1[...] + h2[...] + h3[...]
    for rows, out in ((slice(0, 32), keep), (slice(32, 64), low)):
        out[:, 0:3072] = first[rows, :]
        out[:, 3072:4096] = h[rows, :]


def part_kernel(keep, got, own, over):
    for m in range(4):
        for half, out in enumerate((own, over)):
            cols = slice(m * 1024 + half * 512, m * 1024 + half * 512 + 512)
            out[:, m * 512:m * 512 + 512] = keep[:, cols] + got[:, cols]


def final_kernel(at, own, got, h_out, s_out):
    mz, mx, y_lo, y_hi, core = where_am_i(at)
    for src, col_half in ((own, y_hi), (got, 1 - y_hi)):
        for m, out, h in ((0, h_out, col_half), (1, s_out, col_half), (2, s_out, 1 - col_half), (3, h_out, 1 - col_half)):
            rows = pl.ds(pl.multiple_of(h * 32, 32), 32)
            for n in range(2):
                for c in range(2):
                    cols = pl.ds(pl.multiple_of((col_half * 2 + (core ^ c)) * 128, 128), 128)
                    base = m * 512 + n * 256 + c * 128
                    out[n, rows, cols] = src[:, base:base + 128]


def after(value, *earlier):
    return lax.optimization_barrier((value, *earlier))[0]


def after_all(values, *earlier):
    return list(lax.optimization_barrier((*values, *earlier))[:len(values)])


def shards(psi, hpsi, rot):
    band = lax.axis_index("band")
    ga = lax.axis_index("ga")
    y_hi, core = band >> 1, band & 1
    mz, mx, y_lo = ga >> 3, (ga >> 1) & 3, ga & 1
    at = jnp.stack([mz, mx, y_lo, y_hi, core]).astype(jnp.int32)

    def lefts(both, *blocks):
        count = 8 if both else 4
        return call(functools.partial(left_kernel, both), [jax.ShapeDtypeStruct((256, 1536), jnp.bfloat16)] * count,
                    at, *blocks, in_specs=[SMEM] + [VMEM] * len(blocks), out_specs=[VMEM] * count)

    def for_peer(left, operand, factor):
        return (dot_rows(left, operand) * factor).astype(jnp.float16)

    def gathered(mine, operand, factors, got):
        total = dot_rows(mine, operand)
        for factor, g in zip(factors, got):
            total = total + g.astype(jnp.float32) * factor
        return total

    fence = lax.optimization_barrier

    largest = jnp.stack([jnp.max(jnp.abs(psi)), jnp.max(jnp.abs(hpsi))]).astype(jnp.float32)
    rot_other = move(rot, y_lo=1)
    psi_mate = move(psi, core=1)
    hpsi_mate = move(hpsi, core=1)
    psi, hpsi, psi_mate, hpsi_mate, rot_other = fence((psi, hpsi, psi_mate, hpsi_mate, rot_other))

    sent = call(split_kernel, [jax.ShapeDtypeStruct((2, 2, 80, 128), jnp.bfloat16)] * 4, at, largest, rot,
                rot_other, in_specs=[SMEM, SMEM, VMEM, VMEM], out_specs=[VMEM] * 4)
    got = [sent[0], move(sent[1], core=1), move(sent[2], y_hi=1), move(sent[3], core=1, y_hi=1)]
    right = call(right_kernel, jax.ShapeDtypeStruct((2048, 1536), jnp.bfloat16), at, psi, psi_mate,
                 after(hpsi, sent[0]), hpsi_mate, limit=32, in_specs=[SMEM] + [VMEM] * 4, out_specs=VMEM)
    near_left = lefts(False, after(psi, right), psi_mate)
    psi, hpsi, got, right, near_left = fence((psi, hpsi, got, right, near_left))

    turned, scale = call(turn_kernel, [jax.ShapeDtypeStruct((528, 256), jnp.bfloat16),
                                       jax.ShapeDtypeStruct((8, 2048), jnp.float32)], at, *got,
                         in_specs=[SMEM] + [VMEM] * 4, out_specs=[VMEM] * 2)
    scale = scale[0:1]
    scale_h, scale_s = scale[:, 0:1024], scale[:, 1024:2048]
    cross_a = move(psi[:, :, 0:256], y_hi=1)
    xs = [turned, move(turned, dx=-1), move(turned, dx=2), move(turned, dx=1)]
    near_1 = for_peer(after(near_left[1], turned), right, scale)
    near_3 = for_peer(after(near_left[3], near_1), right, scale)
    psi, hpsi, cross_a, near_1, near_3, right = fence((psi, hpsi, cross_a, near_1, near_3, right))
    xs, right = fence((xs, right))

    mine = call(merge_kernel, jax.ShapeDtypeStruct((528, 1024), jnp.bfloat16), at, *xs,
                in_specs=[SMEM] + [VMEM] * 4, out_specs=VMEM,
                scratch_shapes=[pltpu.VMEM((4, 528, 256), jnp.bfloat16)])
    near_got = [move(near_1, dx=1), move(near_3, dx=3)]
    up, down = move(mine, dz=-1), move(mine, dz=1)
    cross_b = move(psi[:, :, 256:768], y_hi=1)
    near_2 = for_peer(after(near_left[2], mine), right, scale)
    near_own = dot_rows(after(near_left[0], near_2), right)
    hpsi, cross_a, mine, up, down, near_got, near_2, near_own, right = fence(
        (hpsi, cross_a, mine, up, down, near_got, near_2, near_own, right))
    cross_b, near_2, up, down = fence((cross_b, near_2, up, down))

    mate_a, mate_b = move(cross_a, core=1), move(cross_b, core=1)
    near_got.append(move(near_2, dx=2))
    down_half, up_half = down[:, 0:512], up[:, 512:1024]
    far0, far1 = move(down_half, dz=1), move(up_half, dz=-1)
    hpsi_cross = move(hpsi, y_hi=1)
    psi_cross, psi_cross_mate = [cross_a, cross_b], [mate_a, mate_b]
    away_left = lefts(True, *psi_cross, *psi_cross_mate)
    right_h, right_s = right[0:1024], right[1024:2048]
    h_2 = for_peer(away_left[6], right_h, scale_h)
    got_h = [move(h_2, dz=2)]
    h_1 = for_peer(after(away_left[5], h_2), right_h, scale_h)
    h_3 = for_peer(after(away_left[7], h_1), right_h, scale_h)
    s_1 = for_peer(after(away_left[1], h_3), right_s, scale_s)
    s_3 = for_peer(after(away_left[3], s_1), right_s, scale_s)
    s_2 = for_peer(after(away_left[2], s_3), right_s, scale_s)
    psi_near = rotate(at, after_all([mine, up, down], s_2), [psi, psi_mate])
    hpsi_near = rotate(at, after_all([mine, up, down], psi_near), [hpsi, hpsi_mate])
    coef = [mine, up, down, far0, far1]
    near_got, coef, h_1, h_3, s_1, s_3, s_2, got_h, right, away_left, psi_near, hpsi_near = fence(
        (near_got, coef, h_1, h_3, s_1, s_3, s_2, got_h, right, away_left, psi_near, hpsi_near))

    right_h, right_s = right[0:1024], right[1024:2048]
    got_h += [move(h_1, dz=1), move(h_3, dz=3)]
    got_s = [move(s_1, dx=1), move(s_3, dx=3), move(s_2, dx=2)]
    rotated_psi = rotate(at, coef, [psi, psi_mate, psi_cross, psi_cross_mate], psi_near)
    factors = call(factor_kernel, jax.ShapeDtypeStruct((16, 2048), jnp.float32), after(at, rotated_psi), *xs[1:], mine, up,
                   far0, down, in_specs=[SMEM] + [VMEM] * 7, out_specs=VMEM)
    hpsi_cross, got_h, got_s, near_got, near_own, rotated_psi, factors, right = fence(
        (hpsi_cross, got_h, got_s, near_got, near_own, rotated_psi, factors, right))

    right_h, right_s = right[0:1024], right[1024:2048]
    factor = [factors[n:n + 1] for n in range(10)]
    got_h = [got_h[1], got_h[2], got_h[0]]
    away_h = gathered(away_left[4], right_h, [f[:, 0:1024] for f in factor[3:6]], got_h)
    by_x = [away_h[0:64]] + [move(away_h[d * 64:d * 64 + 64], dx=d) for d in (1, 3, 2)]
    near_total = after(near_own, away_h)
    for n, g in enumerate(near_got):
        near_total = near_total + g.astype(jnp.float32) * factor[n]
    away_s = gathered(after(away_left[0], near_total), right_s, [f[:, 1024:2048] for f in factor[0:3]], got_s)
    hpsi_cross_mate = move(hpsi_cross, core=1)
    by_z = jnp.concatenate([near_total, away_s], axis=1)
    factor = [jnp.concatenate([f, f[:, 1024:2048]], axis=1) for f in factor[6:10]]
    by_z = [by_z[0:64]] + [move((by_z[d * 64:d * 64 + 64] * factor[0]).astype(jnp.float16), dz=d) for d in (1, 3, 2)]
    first = by_z[0]
    for p, f in zip(by_z[1:], factor[1:]):
        first = first + p.astype(jnp.float32) * f
    keep, low = call(fold_kernel, [jax.ShapeDtypeStruct((32, 4096), jnp.float32)] * 2, first, *by_x,
                     in_specs=[VMEM] * 5, out_specs=[VMEM] * 2)
    low_got = move(low, y_lo=1)
    blocks = [hpsi, hpsi_mate, hpsi_cross, hpsi_cross_mate]
    part_1 = rotate(at, after_all(coef, low), blocks, hpsi_near, rows=0)
    own, over = call(part_kernel, [jax.ShapeDtypeStruct((32, 2048), jnp.float32)] * 2, after(keep, part_1),
                     low_got, in_specs=[VMEM] * 2, out_specs=[VMEM] * 2)
    rotated_hpsi = rotate(at, after_all(coef, over), blocks, part_1, rows=1)
    own = after(own, rotated_hpsi)
    half = jax.ShapeDtypeStruct((2, 64, 512), jnp.float32)
    subspace_h, correlation_s = call(
        final_kernel, [half, half], at, own, move(over, y_hi=1), in_specs=[SMEM] + [VMEM] * 2, out_specs=[VMEM] * 2)
    return rotated_psi, rotated_hpsi, subspace_h, correlation_s


def solution(mesh):
    placed = (P(None, "band", "ga"), P(None, "band", "ga"), P(None, "ga", "band"))
    return jax.shard_map(
        shards,
        mesh=mesh,
        in_specs=placed,
        out_specs=(
            P(None, "band", "ga"),
            P(None, "band", "ga"),
            P(None, "ga", "band"),
            P(None, "ga", "band"),
        ),
        check_vma=False,
    )
```

```python
import functools

import jax
import jax.numpy as jnp
from jax import lax
from jax.experimental import pallas as pl
from jax.experimental.pallas import tpu as pltpu
from jax.sharding import PartitionSpec as P

ROOM = 8192.0
TINY = 1e-30
MIB = 1024 * 1024
VMEM = pl.BlockSpec(memory_space=pltpu.VMEM)
SMEM = pl.BlockSpec(memory_space=pltpu.SMEM)


def place(device):
    band, ga = divmod(device, 32)
    y_hi, core = divmod(band, 2)
    z, rest = divmod(ga, 8)
    x, y_lo = divmod(rest, 2)
    return [z, x, y_lo, y_hi, core]


def device_at(z, x, y_lo, y_hi, core):
    return (y_hi * 2 + core) * 32 + z * 8 + x * 2 + y_lo


def move(value, dz=0, dx=0, y_lo=0, y_hi=0, core=0):
    pairs = []
    for source in range(128):
        z, x, low, high, c = place(source)
        target = device_at((z + dz) % 4, (x + dx) % 4, low ^ y_lo, high ^ y_hi, c ^ core)
        pairs.append((source, target))
    return lax.ppermute(value, ("band", "ga"), pairs)


def dot_rows(left, right):
    return lax.dot_general(left, right, (((1,), (1,)), ((), ())), preferred_element_type=jnp.float32)


def where_am_i(at):
    return at[0], at[1], at[2], at[3], at[4]


def call(kernel, outs, *args, limit=24, **kw):
    return pl.pallas_call(
        kernel,
        out_shape=outs,
        compiler_params=pltpu.CompilerParams(vmem_limit_bytes=limit * MIB),
        cost_estimate=pl.CostEstimate(flops=1024, bytes_accessed=1024, transcendentals=0),
        **kw,
    )(*args)


def largest_kernel(psi, hpsi, out):
    for m, ref in enumerate((psi, hpsi)):
        most = jnp.abs(ref[0, 0:16, :])
        for c in range(2):
            for n in range(32):
                most = jnp.maximum(most, jnp.abs(ref[c, n * 16:n * 16 + 16, :]))
        out[m] = jnp.max(most.astype(jnp.float32))


def split_kernel(at, largest, own, other, first, second, third, fourth):
    mz, mx, y_lo, y_hi, core = where_am_i(at)
    for k, out in enumerate((first, second, third, fourth)):
        band = (y_hi * 2 + core) ^ k
        cols = pl.ds(pl.multiple_of(band * 128, 128), 128)
        out[y_lo, :, 0:64, :] = own[:, :, cols]
        out[1 - y_lo, :, 0:64, :] = other[:, :, cols]
        tail = jnp.concatenate([jnp.full((8, 128), largest[0], jnp.float32), jnp.full((8, 128), largest[1], jnp.float32)])
        for low in range(2):
            for c in range(2):
                out[low, c, 64:80, :] = tail.astype(jnp.bfloat16)


def turn_kernel(at, first, second, third, fourth, out, scales):
    mz, mx, y_lo, y_hi, core = where_am_i(at)
    tails = []
    for k, src in enumerate((first, second, third, fourth)):
        band = (y_hi * 2 + core) ^ k
        rows = jnp.concatenate(
            [src[low, c, h * 32:h * 32 + 32, :] for h in range(2) for c in range(2) for low in range(2)], axis=0)
        turned = rows.astype(jnp.float32).T.astype(jnp.bfloat16)
        for g in range(4):
            out[pl.ds(pl.multiple_of(g * 128 + band * 32, 32), 32), :] = turned[g * 32:g * 32 + 32, :]
        tails.append(src[0, 0, 64:80, :].astype(jnp.float32))
    chip = jnp.maximum(tails[0], tails[1])
    psi = jnp.maximum(chip, jnp.maximum(tails[2], tails[3]))[0:8]
    for m, right in ((0, chip[8:16]), (1, chip[0:8])):
        factor = (ROOM / (1536.0 * psi * right + TINY)).astype(jnp.bfloat16).astype(jnp.float32)
        for n in range(8):
            scales[:, m * 1024 + n * 128:m * 1024 + n * 128 + 128] = factor
        if m == 0:
            first_factor = factor
    tail = jnp.concatenate([first_factor, factor], axis=0).astype(jnp.bfloat16)
    out[512:528, 0:128] = tail
    out[512:528, 128:256] = tail


def factor_kernel(at, x1, x2, x3, mine, up, far, down, out):
    mz, mx, y_lo, y_hi, core = where_am_i(at)
    lanes = lax.broadcasted_iota(jnp.int32, (16, 256), 1)

    def put(row, pair):
        for m in range(2):
            out[row:row + 1, m * 1024:m * 1024 + 1024] = jnp.broadcast_to(pair[m], (1, 1024))

    def pair(values):
        return values[0:1, 0:1], values[8:9, 0:1]

    for row, ref in enumerate((x3, x1, x2)):
        put(row, [1.0 / v for v in pair(ref[512:528, 0:128].astype(jnp.float32))])
    for row, ref in enumerate((down, up, far)):
        values = ref[512:528, 0:256].astype(jnp.float32)
        here = jnp.min(jnp.where((lanes >> 6) == mx, values, 3e38), axis=1, keepdims=True)
        put(3 + row, [1.0 / v for v in pair(here)])
        put(7 + row, [1.0 / v for v in pair(jnp.min(values, axis=1, keepdims=True))])
    put(6, pair(jnp.min(mine[512:528, 0:256].astype(jnp.float32), axis=1, keepdims=True)))


def merge_kernel(at, first, second, third, fourth, out, pieces):
    mz, mx, y_lo, y_hi, core = where_am_i(at)
    for d, src in enumerate((first, second, third, fourth)):
        pieces[d] = src[...]
    for part in range(4):
        blocks = [pieces[(x - mx) & 3, :, part * 64:part * 64 + 64] for x in range(4)]
        out[:, part * 256:part * 256 + 256] = jnp.concatenate(blocks, axis=1)


def right_kernel(at, psi, psi_mate, hpsi, hpsi_mate, out):
    mz, mx, y_lo, y_hi, core = where_am_i(at)
    for half in range(2):
        band = (y_hi ^ half) * 2 + core
        for m, pair in enumerate(((hpsi, hpsi_mate), (psi, psi_mate))):
            for c, src in enumerate(pair):
                for g in range(4):
                    rows = pl.ds(pl.multiple_of(g * 128 + band * 32, 32), 32)
                    re, im = src[0, rows, :], src[1, rows, :]
                    base = m * 1024 + half * 512 + c * 128 + g * 32
                    out[base:base + 32, 0:768] = re
                    out[base:base + 32, 768:1536] = im
                    out[base + 256:base + 288, 0:768] = im
                    out[base + 256:base + 288, 768:1536] = -re


def left_kernel(both, at, *refs):
    mz, mx, y_lo, y_hi, core = where_am_i(at)
    pieces = 2 if both else 1
    nears, others, outs = refs[:pieces], refs[pieces:2 * pieces], refs[2 * pieces:]
    for dz in range(4):
        z = (mz + dz) & 3
        is_near = (z >> 1) == core
        for dx in range(4):
            x = (mx + dx) & 3
            for dy in range(2):
                rows = pl.ds(pl.multiple_of((z & 1) * 256 + x * 64 + (y_lo ^ dy) * 32, 32), 32)
                by_x, by_z = dz * 64 + dy * 32, dx * 64 + dy * 32
                for c in range(2):
                    base = c * 768
                    for near, other in zip(nears, others):
                        value = jnp.where(is_near, near[c, rows, :], other[c, rows, :])
                        cols = slice(base, base + value.shape[1])
                        base += value.shape[1]
                        outs[dx][by_x:by_x + 32, cols] = value
                        if both:
                            outs[4 + dz][by_z:by_z + 32, cols] = value


def planes(refs):
    return lambda c, rows: refs[c][rows, :]


def columns(refs):
    return lambda c, rows: jnp.concatenate([r[c, rows, :] for r in refs], axis=1)


def own_kernel(left_h, left_s, right, out_h, out_s):
    out_h[...] = dot_rows(left_h[...], right[0:1024, :])
    out_s[...] = dot_rows(left_s[...], right[1024:2048, :])


def rotate_kernel(early, split, at, z0, z1, z3, *refs):
    mz, mx, y_lo, y_hi, core = where_am_i(at)
    out = refs[-1]
    if early:
        near, other = planes(refs[0:2]), planes(refs[2:4])
        pairs = ((y_hi, near, other, ((0, z0), (1, z1), (3, z3))),)
        total = None
    else:
        far0, far1, acc = refs[0], refs[1], refs[10]
        near, other = planes(refs[2:4]), planes(refs[4:6])
        cross = (columns if split else planes)(refs[6:8]), (columns if split else planes)(refs[8:10])
        pairs = ((y_hi, near, other, ((2, None),)),
                 (1 - y_hi, *cross, ((0, z0), (1, z1), (2, None), (3, z3))))
        total = jnp.concatenate([acc[0], acc[1]], axis=0)
    for h, near, other, pieces in pairs:
        for dz, piece in pieces:
            z = (mz + dz) & 3
            is_near = (z >> 1) == core
            rows = pl.ds(pl.multiple_of((z & 1) * 256, 256), 256)
            if piece is None:
                coef = jnp.where(h == 0, far0[...], far1[...])
                re, im = coef[:, 0:256], coef[:, 256:512]
            else:
                re = piece[:, pl.ds(pl.multiple_of(h * 512, 512), 256)]
                im = piece[:, pl.ds(pl.multiple_of(h * 512 + 256, 256), 256)]
            left = jnp.concatenate([
                jnp.concatenate([re, -im], axis=1),
                jnp.concatenate([im, re], axis=1),
            ], axis=0)
            right = jnp.concatenate([
                jnp.where(is_near, near(0, rows), other(0, rows)),
                jnp.where(is_near, near(1, rows), other(1, rows)),
            ], axis=0)
            term = jnp.dot(left, right, preferred_element_type=jnp.float32)
            total = term if total is None else total + term
    size = total.shape[0] // 2
    for part in range(2):
        out[part] = total[part * size:part * size + size]


def rotate(at, pieces, blocks, acc=None, rows=None):
    step = 256
    first, steps = (0, 512 // step) if rows is None else (rows * 256 // step, 256 // step)
    tile = pl.BlockSpec((2, step, 768), lambda n: (0, n + first, 0))
    plane = [pl.BlockSpec((pl.squeezed, 512, 768), lambda n, c=c: (c, 0, 0)) for c in range(2)]
    args = [at, *pieces]
    specs = [SMEM] + [pl.BlockSpec((step, c.shape[1]), lambda n: (n + first, 0)) for c in pieces]
    for block in blocks:
        args += block if isinstance(block, list) else [block, block]
        specs += [VMEM, VMEM] if isinstance(block, list) else plane
    if acc is not None:
        args.append(acc)
        specs.append(tile)
    return call(
        functools.partial(rotate_kernel, acc is None, isinstance(blocks[-1], list)),
        jax.ShapeDtypeStruct((2, 512, 768), jnp.float32),
        *args,
        limit=20 if acc is None else 32,
        grid=(steps,),
        in_specs=specs,
        out_specs=tile,
        input_output_aliases={} if rows is None else {len(args) - 1: 0},
    )


def fold_kernel(first, h, keep, low):
    for rows, out in ((slice(0, 32), keep), (slice(32, 64), low)):
        out[:, 0:3072] = first[rows, :]
        out[:, 3072:4096] = h[rows, :]


def part_kernel(keep, got, own, over):
    for m in range(4):
        for half, out in enumerate((own, over)):
            cols = slice(m * 1024 + half * 512, m * 1024 + half * 512 + 512)
            out[:, m * 512:m * 512 + 512] = keep[:, cols] + got[:, cols]


def final_kernel(at, own, got, h_out, s_out):
    mz, mx, y_lo, y_hi, core = where_am_i(at)
    for src, col_half in ((own, y_hi), (got, 1 - y_hi)):
        for m, out, h in ((0, h_out, col_half), (1, s_out, col_half), (2, s_out, 1 - col_half), (3, h_out, 1 - col_half)):
            rows = pl.ds(pl.multiple_of(h * 32, 32), 32)
            for n in range(2):
                for c in range(2):
                    cols = pl.ds(pl.multiple_of((col_half * 2 + (core ^ c)) * 128, 128), 128)
                    base = m * 512 + n * 256 + c * 128
                    out[n, rows, cols] = src[:, base:base + 128]


def after(value, *earlier):
    return lax.optimization_barrier((value, *earlier))[0]


def after_all(values, *earlier):
    return list(lax.optimization_barrier((*values, *earlier))[:len(values)])


def shards(psi, hpsi, rot):
    band = lax.axis_index("band")
    ga = lax.axis_index("ga")
    y_hi, core = band >> 1, band & 1
    mz, mx, y_lo = ga >> 3, (ga >> 1) & 3, ga & 1
    at = jnp.stack([mz, mx, y_lo, y_hi, core]).astype(jnp.int32)

    def lefts(both, *blocks):
        count = 8 if both else 4
        return call(functools.partial(left_kernel, both), [jax.ShapeDtypeStruct((256, 1536), jnp.bfloat16)] * count,
                    at, *blocks, in_specs=[SMEM] + [VMEM] * len(blocks), out_specs=[VMEM] * count)

    def for_peer(left, operand, factor):
        return (dot_rows(left, operand) * factor).astype(jnp.float16)

    def gathered(total, factors, got):
        for factor, g in zip(factors, got):
            total = total + g.astype(jnp.float32) * factor
        return total

    fence = lax.optimization_barrier

    largest = call(largest_kernel, jax.ShapeDtypeStruct((2,), jnp.float32), psi, hpsi,
                   in_specs=[VMEM] * 2, out_specs=SMEM)
    rot_other = move(rot, y_lo=1)
    psi_mate = move(psi, core=1)
    hpsi_mate = move(hpsi, core=1)
    psi, hpsi, psi_mate, hpsi_mate, rot_other = fence((psi, hpsi, psi_mate, hpsi_mate, rot_other))

    sent = call(split_kernel, [jax.ShapeDtypeStruct((2, 2, 80, 128), jnp.bfloat16)] * 4, at, largest, rot,
                rot_other, in_specs=[SMEM, SMEM, VMEM, VMEM], out_specs=[VMEM] * 4)
    got = [sent[0], move(sent[1], core=1), move(sent[2], y_hi=1), move(sent[3], core=1, y_hi=1)]
    right = call(right_kernel, jax.ShapeDtypeStruct((2048, 1536), jnp.bfloat16), at, psi, psi_mate,
                 after(hpsi, sent[0]), hpsi_mate, limit=32, in_specs=[SMEM] + [VMEM] * 4, out_specs=VMEM)
    near_left = lefts(False, after(psi, right), psi_mate)
    psi, hpsi, got, right, near_left = fence((psi, hpsi, got, right, near_left))

    turned, scale = call(turn_kernel, [jax.ShapeDtypeStruct((528, 256), jnp.bfloat16),
                                       jax.ShapeDtypeStruct((8, 2048), jnp.float32)], at, *got,
                         in_specs=[SMEM] + [VMEM] * 4, out_specs=[VMEM] * 2)
    scale = scale[0:1]
    scale_h, scale_s = scale[:, 0:1024], scale[:, 1024:2048]
    cross_a = move(psi[:, :, 0:256], y_hi=1)
    xs = [turned, move(turned, dx=-1), move(turned, dx=2), move(turned, dx=1)]
    near_1 = for_peer(after(near_left[1], turned), right, scale)
    near_3 = for_peer(after(near_left[3], near_1), right, scale)
    psi, hpsi, cross_a, near_1, near_3, right = fence((psi, hpsi, cross_a, near_1, near_3, right))
    xs, right = fence((xs, right))

    mine = call(merge_kernel, jax.ShapeDtypeStruct((528, 1024), jnp.bfloat16), at, *xs,
                in_specs=[SMEM] + [VMEM] * 4, out_specs=VMEM,
                scratch_shapes=[pltpu.VMEM((4, 528, 256), jnp.bfloat16)])
    near_got = [move(near_1, dx=1), move(near_3, dx=3)]
    up, down = move(mine, dz=-1), move(mine, dz=1)
    cross_b = move(psi[:, :, 256:768], y_hi=1)
    near_2 = for_peer(after(near_left[2], mine), right, scale)
    near_own = dot_rows(after(near_left[0], near_2), right)
    hpsi, cross_a, mine, up, down, near_got, near_2, near_own, right = fence(
        (hpsi, cross_a, mine, up, down, near_got, near_2, near_own, right))
    cross_b, near_2, up, down = fence((cross_b, near_2, up, down))

    mate_a, mate_b = move(cross_a, core=1), move(cross_b, core=1)
    near_got.append(move(near_2, dx=2))
    down_half, up_half = down[:, 0:512], up[:, 512:1024]
    far0, far1 = move(down_half, dz=1), move(up_half, dz=-1)
    hpsi_cross = move(hpsi, y_hi=1)
    psi_cross, psi_cross_mate = [cross_a, cross_b], [mate_a, mate_b]
    away_left = lefts(True, *psi_cross, *psi_cross_mate)
    right_h, right_s = right[0:1024], right[1024:2048]
    h_2 = for_peer(away_left[6], right_h, scale_h)
    got_h = [move(h_2, dz=2)]
    h_1 = for_peer(after(away_left[5], h_2), right_h, scale_h)
    h_3 = for_peer(after(away_left[7], h_1), right_h, scale_h)
    s_1 = for_peer(after(away_left[1], h_3), right_s, scale_s)
    s_3 = for_peer(after(away_left[3], s_1), right_s, scale_s)
    s_2 = for_peer(after(away_left[2], s_3), right_s, scale_s)
    psi_near = rotate(at, after_all([mine, up, down], s_2), [psi, psi_mate])
    hpsi_near = rotate(at, after_all([mine, up, down], psi_near), [hpsi, hpsi_mate])
    coef = [mine, up, down, far0, far1]
    near_got, coef, h_1, h_3, s_1, s_3, s_2, got_h, right, away_left, psi_near, hpsi_near = fence(
        (near_got, coef, h_1, h_3, s_1, s_3, s_2, got_h, right, away_left, psi_near, hpsi_near))

    right_h, right_s = right[0:1024], right[1024:2048]
    got_h += [move(h_1, dz=1), move(h_3, dz=3)]
    got_s = [move(s_1, dx=1), move(s_3, dx=3), move(s_2, dx=2)]
    rotated_psi = rotate(at, coef, [psi, psi_mate, psi_cross, psi_cross_mate], psi_near)
    factors = call(factor_kernel, jax.ShapeDtypeStruct((16, 2048), jnp.float32), after(at, rotated_psi), *xs[1:], mine, up,
                   far0, down, in_specs=[SMEM] + [VMEM] * 7, out_specs=VMEM)
    own_h, own_s = call(own_kernel, [jax.ShapeDtypeStruct((256, 1024), jnp.float32)] * 2, after(away_left[4], factors),
                        away_left[0], right, in_specs=[VMEM] * 3, out_specs=[VMEM] * 2)
    hpsi_cross, got_h, got_s, near_got, near_own, rotated_psi, factors, own_h, own_s = fence(
        (hpsi_cross, got_h, got_s, near_got, near_own, rotated_psi, factors, own_h, own_s))

    factor = [factors[n:n + 1] for n in range(10)]
    got_h = [got_h[1], got_h[2], got_h[0]]
    away_h = gathered(own_h, [f[:, 0:1024] for f in factor[3:6]], got_h)
    by_x = [away_h[0:64]] + [move(away_h[d * 64:d * 64 + 64], dx=d) for d in (1, 3, 2)]
    near_total = after(near_own, away_h)
    for n, g in enumerate(near_got):
        near_total = near_total + g.astype(jnp.float32) * factor[n]
    away_s = gathered(after(own_s, near_total), [f[:, 1024:2048] for f in factor[0:3]], got_s)
    hpsi_cross_mate = move(hpsi_cross, core=1)
    by_z = jnp.concatenate([near_total, away_s], axis=1)
    factor = [jnp.concatenate([f, f[:, 1024:2048]], axis=1) for f in factor[6:10]]
    by_z = [by_z[0:64]] + [move((by_z[d * 64:d * 64 + 64] * factor[0]).astype(jnp.float16), dz=d) for d in (1, 3, 2)]
    sum_h = by_x[0] + by_x[1] + by_x[2] + by_x[3]
    first = after(by_z[0], sum_h)
    for p, f in zip(by_z[1:], factor[1:]):
        first = first + p.astype(jnp.float32) * f
    keep, low = call(fold_kernel, [jax.ShapeDtypeStruct((32, 4096), jnp.float32)] * 2, first, sum_h,
                     in_specs=[VMEM] * 2, out_specs=[VMEM] * 2)
    low_got = move(low, y_lo=1)
    blocks = [hpsi, hpsi_mate, hpsi_cross, hpsi_cross_mate]
    part_1 = rotate(at, after_all(coef, low), blocks, hpsi_near, rows=0)
    own, over = call(part_kernel, [jax.ShapeDtypeStruct((32, 2048), jnp.float32)] * 2, after(keep, part_1),
                     low_got, in_specs=[VMEM] * 2, out_specs=[VMEM] * 2)
    rotated_hpsi = rotate(at, after_all(coef, over), blocks, part_1, rows=1)
    own = after(own, rotated_hpsi)
    half = jax.ShapeDtypeStruct((2, 64, 512), jnp.float32)
    subspace_h, correlation_s = call(
        final_kernel, [half, half], at, own, move(over, y_hi=1), in_specs=[SMEM] + [VMEM] * 2, out_specs=[VMEM] * 2)
    return rotated_psi, rotated_hpsi, subspace_h, correlation_s


def solution(mesh):
    placed = (P(None, "band", "ga"), P(None, "band", "ga"), P(None, "ga", "band"))
    return jax.shard_map(
        shards,
        mesh=mesh,
        in_specs=placed,
        out_specs=(
            P(None, "band", "ga"),
            P(None, "band", "ga"),
            P(None, "ga", "band"),
            P(None, "ga", "band"),
        ),
        check_vma=False,
    )
```

```python
import functools

import jax
import jax.numpy as jnp
from jax import lax
from jax.experimental import pallas as pl
from jax.experimental.pallas import tpu as pltpu
from jax.sharding import PartitionSpec as P

ROOM = 8192.0
TINY = 1e-30
MIB = 1024 * 1024
VMEM = pl.BlockSpec(memory_space=pltpu.VMEM)
SMEM = pl.BlockSpec(memory_space=pltpu.SMEM)


def place(device):
    band, ga = divmod(device, 32)
    y_hi, core = divmod(band, 2)
    z, rest = divmod(ga, 8)
    x, y_lo = divmod(rest, 2)
    return [z, x, y_lo, y_hi, core]


def device_at(z, x, y_lo, y_hi, core):
    return (y_hi * 2 + core) * 32 + z * 8 + x * 2 + y_lo


def move(value, dz=0, dx=0, y_lo=0, y_hi=0, core=0):
    pairs = []
    for source in range(128):
        z, x, low, high, c = place(source)
        target = device_at((z + dz) % 4, (x + dx) % 4, low ^ y_lo, high ^ y_hi, c ^ core)
        pairs.append((source, target))
    return lax.ppermute(value, ("band", "ga"), pairs)


def dot_rows(left, right):
    return lax.dot_general(left, right, (((1,), (1,)), ((), ())), preferred_element_type=jnp.float32)


def where_am_i(at):
    return at[0], at[1], at[2], at[3], at[4]


def call(kernel, outs, *args, limit=24, **kw):
    return pl.pallas_call(
        kernel,
        out_shape=outs,
        compiler_params=pltpu.CompilerParams(vmem_limit_bytes=limit * MIB),
        cost_estimate=pl.CostEstimate(flops=1024, bytes_accessed=1024, transcendentals=0),
        **kw,
    )(*args)


def largest_kernel(psi, hpsi, out):
    for m, ref in enumerate((psi, hpsi)):
        most = jnp.abs(ref[0, 0:16, :])
        for c in range(2):
            for n in range(32):
                most = jnp.maximum(most, jnp.abs(ref[c, n * 16:n * 16 + 16, :]))
        out[m] = jnp.max(most.astype(jnp.float32))


def split_kernel(at, largest, own, other, first, second, third, fourth):
    mz, mx, y_lo, y_hi, core = where_am_i(at)
    for k, out in enumerate((first, second, third, fourth)):
        band = (y_hi * 2 + core) ^ k
        cols = pl.ds(pl.multiple_of(band * 128, 128), 128)
        out[y_lo, :, 0:64, :] = own[:, :, cols]
        out[1 - y_lo, :, 0:64, :] = other[:, :, cols]
        tail = jnp.concatenate([jnp.full((8, 128), largest[0], jnp.float32), jnp.full((8, 128), largest[1], jnp.float32)])
        for low in range(2):
            for c in range(2):
                out[low, c, 64:80, :] = tail.astype(jnp.bfloat16)


def turn_kernel(at, first, second, third, fourth, out, scales):
    mz, mx, y_lo, y_hi, core = where_am_i(at)
    tails = []
    for k, src in enumerate((first, second, third, fourth)):
        band = (y_hi * 2 + core) ^ k
        rows = jnp.concatenate(
            [src[low, c, h * 32:h * 32 + 32, :] for h in range(2) for c in range(2) for low in range(2)], axis=0)
        turned = rows.astype(jnp.float32).T.astype(jnp.bfloat16)
        for g in range(4):
            out[pl.ds(pl.multiple_of(g * 128 + band * 32, 32), 32), :] = turned[g * 32:g * 32 + 32, :]
        tails.append(src[0, 0, 64:80, :].astype(jnp.float32))
    chip = jnp.maximum(tails[0], tails[1])
    psi = jnp.maximum(chip, jnp.maximum(tails[2], tails[3]))[0:8]
    for m, right in ((0, chip[8:16]), (1, chip[0:8])):
        factor = (ROOM / (1536.0 * psi * right + TINY)).astype(jnp.bfloat16).astype(jnp.float32)
        for n in range(8):
            scales[:, m * 1024 + n * 128:m * 1024 + n * 128 + 128] = factor
        if m == 0:
            first_factor = factor
    tail = jnp.concatenate([first_factor, factor], axis=0).astype(jnp.bfloat16)
    out[512:528, 0:128] = tail
    out[512:528, 128:256] = tail


def factor_kernel(at, x1, x2, x3, mine, up, far, down, out):
    mz, mx, y_lo, y_hi, core = where_am_i(at)
    lanes = lax.broadcasted_iota(jnp.int32, (16, 256), 1)

    def put(row, pair):
        for m in range(2):
            out[row:row + 1, m * 1024:m * 1024 + 1024] = jnp.broadcast_to(pair[m], (1, 1024))

    def pair(values):
        return values[0:1, 0:1], values[8:9, 0:1]

    for row, ref in enumerate((x3, x1, x2)):
        put(row, [1.0 / v for v in pair(ref[512:528, 0:128].astype(jnp.float32))])
    for row, ref in enumerate((down, up, far)):
        values = ref[512:528, 0:256].astype(jnp.float32)
        here = jnp.min(jnp.where((lanes >> 6) == mx, values, 3e38), axis=1, keepdims=True)
        put(3 + row, [1.0 / v for v in pair(here)])
        put(7 + row, [1.0 / v for v in pair(jnp.min(values, axis=1, keepdims=True))])
    put(6, pair(jnp.min(mine[512:528, 0:256].astype(jnp.float32), axis=1, keepdims=True)))


def merge_kernel(at, first, second, third, fourth, out, pieces):
    mz, mx, y_lo, y_hi, core = where_am_i(at)
    for d, src in enumerate((first, second, third, fourth)):
        pieces[d] = src[...]
    for part in range(4):
        blocks = [pieces[(x - mx) & 3, :, part * 64:part * 64 + 64] for x in range(4)]
        out[:, part * 256:part * 256 + 256] = jnp.concatenate(blocks, axis=1)


def right_kernel(at, psi, psi_mate, hpsi, hpsi_mate, out):
    mz, mx, y_lo, y_hi, core = where_am_i(at)
    for half in range(2):
        band = (y_hi ^ half) * 2 + core
        for m, pair in enumerate(((hpsi, hpsi_mate), (psi, psi_mate))):
            for c, src in enumerate(pair):
                for g in range(4):
                    rows = pl.ds(pl.multiple_of(g * 128 + band * 32, 32), 32)
                    re, im = src[0, rows, :], src[1, rows, :]
                    base = m * 1024 + half * 512 + c * 128 + g * 32
                    out[base:base + 32, 0:768] = re
                    out[base:base + 32, 768:1536] = im
                    out[base + 256:base + 288, 0:768] = im
                    out[base + 256:base + 288, 768:1536] = -re


def left_kernel(both, at, *refs):
    mz, mx, y_lo, y_hi, core = where_am_i(at)
    pieces = 2 if both else 1
    nears, others, outs = refs[:pieces], refs[pieces:2 * pieces], refs[2 * pieces:]
    for dz in range(4):
        z = (mz + dz) & 3
        is_near = (z >> 1) == core
        for dx in range(4):
            x = (mx + dx) & 3
            for dy in range(2):
                rows = pl.ds(pl.multiple_of((z & 1) * 256 + x * 64 + (y_lo ^ dy) * 32, 32), 32)
                by_x, by_z = dz * 64 + dy * 32, dx * 64 + dy * 32
                for c in range(2):
                    base = c * 768
                    for near, other in zip(nears, others):
                        value = jnp.where(is_near, near[c, rows, :], other[c, rows, :])
                        cols = slice(base, base + value.shape[1])
                        base += value.shape[1]
                        outs[dx][by_x:by_x + 32, cols] = value
                        if both:
                            outs[4 + dz][by_z:by_z + 32, cols] = value


def planes(refs):
    return lambda c, rows: refs[c][rows, :]


def columns(refs):
    return lambda c, rows: jnp.concatenate([r[c, rows, :] for r in refs], axis=1)


def own_kernel(left_h, left_s, right, out_h, out_s):
    out_h[...] = dot_rows(left_h[...], right[0:1024, :])
    out_s[...] = dot_rows(left_s[...], right[1024:2048, :])


def rotate_kernel(early, split, at, z0, z1, z3, *refs):
    mz, mx, y_lo, y_hi, core = where_am_i(at)
    out = refs[-1]
    if early:
        near, other = planes(refs[0:2]), planes(refs[2:4])
        pairs = ((y_hi, near, other, ((0, z0), (1, z1), (3, z3))),)
        total = None
    else:
        far0, far1, acc = refs[0], refs[1], refs[10]
        near, other = planes(refs[2:4]), planes(refs[4:6])
        cross = (columns if split else planes)(refs[6:8]), (columns if split else planes)(refs[8:10])
        pairs = ((y_hi, near, other, ((2, None),)),
                 (1 - y_hi, *cross, ((0, z0), (1, z1), (2, None), (3, z3))))
        total = jnp.concatenate([acc[0], acc[1]], axis=0)
    for h, near, other, pieces in pairs:
        for dz, piece in pieces:
            z = (mz + dz) & 3
            is_near = (z >> 1) == core
            rows = pl.ds(pl.multiple_of((z & 1) * 256, 256), 256)
            if piece is None:
                coef = jnp.where(h == 0, far0[...], far1[...])
                re, im = coef[:, 0:256], coef[:, 256:512]
            else:
                re = piece[:, pl.ds(pl.multiple_of(h * 512, 512), 256)]
                im = piece[:, pl.ds(pl.multiple_of(h * 512 + 256, 256), 256)]
            left = jnp.concatenate([
                jnp.concatenate([re, -im], axis=1),
                jnp.concatenate([im, re], axis=1),
            ], axis=0)
            right = jnp.concatenate([
                jnp.where(is_near, near(0, rows), other(0, rows)),
                jnp.where(is_near, near(1, rows), other(1, rows)),
            ], axis=0)
            term = jnp.dot(left, right, preferred_element_type=jnp.float32)
            total = term if total is None else total + term
    size = total.shape[0] // 2
    for part in range(2):
        out[part] = total[part * size:part * size + size]


def rotate(at, pieces, blocks, acc=None, rows=None):
    step = 256
    first, steps = (0, 512 // step) if rows is None else (rows * 256 // step, 256 // step)
    tile = pl.BlockSpec((2, step, 768), lambda n: (0, n + first, 0))
    plane = [pl.BlockSpec((pl.squeezed, 512, 768), lambda n, c=c: (c, 0, 0)) for c in range(2)]
    args = [at, *pieces]
    specs = [SMEM] + [pl.BlockSpec((step, c.shape[1]), lambda n: (n + first, 0)) for c in pieces]
    for block in blocks:
        args += block if isinstance(block, list) else [block, block]
        specs += [VMEM, VMEM] if isinstance(block, list) else plane
    if acc is not None:
        args.append(acc)
        specs.append(tile)
    return call(
        functools.partial(rotate_kernel, acc is None, isinstance(blocks[-1], list)),
        jax.ShapeDtypeStruct((2, 512, 768), jnp.float32),
        *args,
        limit=20 if acc is None else 32,
        grid=(steps,),
        in_specs=specs,
        out_specs=tile,
        input_output_aliases={} if rows is None else {len(args) - 1: 0},
    )


def fold_kernel(first, h, keep, low):
    for rows, out in ((slice(0, 32), keep), (slice(32, 64), low)):
        out[:, 0:3072] = first[rows, :]
        out[:, 3072:4096] = h[rows, :]


def part_kernel(keep, got, own, over):
    for m in range(4):
        for half, out in enumerate((own, over)):
            cols = slice(m * 1024 + half * 512, m * 1024 + half * 512 + 512)
            out[:, m * 512:m * 512 + 512] = keep[:, cols] + got[:, cols]


def final_kernel(at, own, got, h_out, s_out):
    mz, mx, y_lo, y_hi, core = where_am_i(at)
    for src, col_half in ((own, y_hi), (got, 1 - y_hi)):
        for m, out, h in ((0, h_out, col_half), (1, s_out, col_half), (2, s_out, 1 - col_half), (3, h_out, 1 - col_half)):
            rows = pl.ds(pl.multiple_of(h * 32, 32), 32)
            for n in range(2):
                for c in range(2):
                    cols = pl.ds(pl.multiple_of((col_half * 2 + (core ^ c)) * 128, 128), 128)
                    base = m * 512 + n * 256 + c * 128
                    out[n, rows, cols] = src[:, base:base + 128]


def after(value, *earlier):
    return lax.optimization_barrier((value, *earlier))[0]


def after_all(values, *earlier):
    return list(lax.optimization_barrier((*values, *earlier))[:len(values)])


def shards(psi, hpsi, rot):
    band = lax.axis_index("band")
    ga = lax.axis_index("ga")
    y_hi, core = band >> 1, band & 1
    mz, mx, y_lo = ga >> 3, (ga >> 1) & 3, ga & 1
    at = jnp.stack([mz, mx, y_lo, y_hi, core]).astype(jnp.int32)

    def lefts(both, *blocks):
        count = 8 if both else 4
        return call(functools.partial(left_kernel, both), [jax.ShapeDtypeStruct((256, 1536), jnp.bfloat16)] * count,
                    at, *blocks, in_specs=[SMEM] + [VMEM] * len(blocks), out_specs=[VMEM] * count)

    def for_peer(left, operand, factor):
        return (dot_rows(left, operand) * factor).astype(jnp.float16)

    def gathered(total, factors, got):
        for factor, g in zip(factors, got):
            total = total + g.astype(jnp.float32) * factor
        return total

    fence = lax.optimization_barrier

    largest = call(largest_kernel, jax.ShapeDtypeStruct((2,), jnp.float32), psi, hpsi,
                   in_specs=[VMEM] * 2, out_specs=SMEM)
    rot_other = move(rot, y_lo=1)
    psi_mate = move(psi, core=1)
    hpsi_mate = move(hpsi, core=1)
    psi, hpsi, psi_mate, hpsi_mate, rot_other = fence((psi, hpsi, psi_mate, hpsi_mate, rot_other))

    sent = call(split_kernel, [jax.ShapeDtypeStruct((2, 2, 80, 128), jnp.bfloat16)] * 4, at, largest, rot,
                rot_other, in_specs=[SMEM, SMEM, VMEM, VMEM], out_specs=[VMEM] * 4)
    got = [sent[0], move(sent[1], core=1), move(sent[2], y_hi=1), move(sent[3], core=1, y_hi=1)]
    right = call(right_kernel, jax.ShapeDtypeStruct((2048, 1536), jnp.bfloat16), at, psi, psi_mate,
                 after(hpsi, sent[0]), hpsi_mate, limit=32, in_specs=[SMEM] + [VMEM] * 4, out_specs=VMEM)
    near_left = lefts(False, after(psi, right), psi_mate)
    psi, hpsi, got, right, near_left = fence((psi, hpsi, got, right, near_left))

    turned, scale = call(turn_kernel, [jax.ShapeDtypeStruct((528, 256), jnp.bfloat16),
                                       jax.ShapeDtypeStruct((8, 2048), jnp.float32)], at, *got,
                         in_specs=[SMEM] + [VMEM] * 4, out_specs=[VMEM] * 2)
    scale = scale[0:1]
    scale_h, scale_s = scale[:, 0:1024], scale[:, 1024:2048]
    cross_a = move(psi[:, :, 0:256], y_hi=1)
    xs = [turned, move(turned, dx=-1), move(turned, dx=2), move(turned, dx=1)]
    near_1 = for_peer(after(near_left[1], turned), right, scale)
    near_3 = for_peer(after(near_left[3], near_1), right, scale)
    psi, hpsi, cross_a, near_1, near_3, right = fence((psi, hpsi, cross_a, near_1, near_3, right))
    xs, right = fence((xs, right))

    mine = call(merge_kernel, jax.ShapeDtypeStruct((528, 1024), jnp.bfloat16), at, *xs,
                in_specs=[SMEM] + [VMEM] * 4, out_specs=VMEM,
                scratch_shapes=[pltpu.VMEM((4, 528, 256), jnp.bfloat16)])
    near_got = [move(near_1, dx=1), move(near_3, dx=3)]
    up, down = move(mine, dz=-1), move(mine, dz=1)
    cross_b = move(psi[:, :, 256:768], y_hi=1)
    near_2 = for_peer(after(near_left[2], mine), right, scale)
    near_own = dot_rows(after(near_left[0], near_2), right)
    cross_b, near_2, near_own = fence((cross_b, near_2, near_own))
    hpsi, cross_a, mine, up, down, near_got, near_2, near_own, right = fence(
        (hpsi, cross_a, mine, up, down, near_got, near_2, near_own, right))

    mate_a, mate_b = move(cross_a, core=1), move(cross_b, core=1)
    near_got.append(move(near_2, dx=2))
    down_half, up_half = down[:, 0:512], up[:, 512:1024]
    far0, far1 = move(down_half, dz=1), move(up_half, dz=-1)
    hpsi_cross = move(hpsi, y_hi=1)
    psi_cross, psi_cross_mate = [cross_a, cross_b], [mate_a, mate_b]
    away_left = lefts(True, *psi_cross, *psi_cross_mate)
    right_h, right_s = right[0:1024], right[1024:2048]
    h_2 = for_peer(away_left[6], right_h, scale_h)
    got_h = [move(h_2, dz=2)]
    h_1 = for_peer(after(away_left[5], h_2), right_h, scale_h)
    h_3 = for_peer(after(away_left[7], h_1), right_h, scale_h)
    s_1 = for_peer(after(away_left[1], h_3), right_s, scale_s)
    s_3 = for_peer(after(away_left[3], s_1), right_s, scale_s)
    s_2 = for_peer(after(away_left[2], s_3), right_s, scale_s)
    psi_near = rotate(at, after_all([mine, up, down], s_2), [psi, psi_mate])
    hpsi_near = rotate(at, after_all([mine, up, down], psi_near), [hpsi, hpsi_mate])
    coef = [mine, up, down, far0, far1]
    near_got, coef, h_1, h_3, s_1, s_3, s_2, got_h, right, away_left, psi_near, hpsi_near = fence(
        (near_got, coef, h_1, h_3, s_1, s_3, s_2, got_h, right, away_left, psi_near, hpsi_near))

    right_h, right_s = right[0:1024], right[1024:2048]
    got_h += [move(h_1, dz=1), move(h_3, dz=3)]
    got_s = [move(s_1, dx=1), move(s_3, dx=3), move(s_2, dx=2)]
    rotated_psi = rotate(at, coef, [psi, psi_mate, psi_cross, psi_cross_mate], psi_near)
    factors = call(factor_kernel, jax.ShapeDtypeStruct((16, 2048), jnp.float32), after(at, rotated_psi), *xs[1:], mine, up,
                   far0, down, in_specs=[SMEM] + [VMEM] * 7, out_specs=VMEM)
    own_h, own_s = call(own_kernel, [jax.ShapeDtypeStruct((256, 1024), jnp.float32)] * 2, after(away_left[4], factors),
                        away_left[0], right, in_specs=[VMEM] * 3, out_specs=[VMEM] * 2)
    hpsi_cross, got_h, got_s, near_got, near_own, rotated_psi, factors, own_h, own_s = fence(
        (hpsi_cross, got_h, got_s, near_got, near_own, rotated_psi, factors, own_h, own_s))

    factor = [factors[n:n + 1] for n in range(10)]
    got_h = [got_h[1], got_h[2], got_h[0]]
    away_h = gathered(own_h, [f[:, 0:1024] for f in factor[3:6]], got_h)
    by_x = [away_h[0:64]] + [move(away_h[d * 64:d * 64 + 64], dx=d) for d in (1, 3, 2)]
    near_total = after(near_own, away_h)
    for n, g in enumerate(near_got):
        near_total = near_total + g.astype(jnp.float32) * factor[n]
    away_s = gathered(after(own_s, near_total), [f[:, 1024:2048] for f in factor[0:3]], got_s)
    hpsi_cross_mate = move(hpsi_cross, core=1)
    by_z = jnp.concatenate([near_total, away_s], axis=1)
    factor = [jnp.concatenate([f, f[:, 1024:2048]], axis=1) for f in factor[6:10]]
    by_z = [by_z[0:64]] + [move((by_z[d * 64:d * 64 + 64] * factor[0]).astype(jnp.float16), dz=d) for d in (1, 3, 2)]
    sum_h = by_x[0] + by_x[1] + by_x[2] + by_x[3]
    first = after(by_z[0], sum_h)
    for p, f in zip(by_z[1:], factor[1:]):
        first = first + p.astype(jnp.float32) * f
    keep, low = call(fold_kernel, [jax.ShapeDtypeStruct((32, 4096), jnp.float32)] * 2, first, sum_h,
                     in_specs=[VMEM] * 2, out_specs=[VMEM] * 2)
    low_got = move(low, y_lo=1)
    blocks = [hpsi, hpsi_mate, hpsi_cross, hpsi_cross_mate]
    part_1 = rotate(at, after_all(coef, low), blocks, hpsi_near, rows=0)
    own, over = call(part_kernel, [jax.ShapeDtypeStruct((32, 2048), jnp.float32)] * 2, after(keep, part_1),
                     low_got, in_specs=[VMEM] * 2, out_specs=[VMEM] * 2)
    rotated_hpsi = rotate(at, after_all(coef, over), blocks, part_1, rows=1)
    own = after(own, rotated_hpsi)
    half = jax.ShapeDtypeStruct((2, 64, 512), jnp.float32)
    subspace_h, correlation_s = call(
        final_kernel, [half, half], at, own, move(over, y_hi=1), in_specs=[SMEM] + [VMEM] * 2, out_specs=[VMEM] * 2)
    return rotated_psi, rotated_hpsi, subspace_h, correlation_s


def solution(mesh):
    placed = (P(None, "band", "ga"), P(None, "band", "ga"), P(None, "ga", "band"))
    return jax.shard_map(
        shards,
        mesh=mesh,
        in_specs=placed,
        out_specs=(
            P(None, "band", "ga"),
            P(None, "band", "ga"),
            P(None, "ga", "band"),
            P(None, "ga", "band"),
        ),
        check_vma=False,
    )
```
